32 devices in a mesh: ref: 8 (over y, x, core), img: 4 (over z).
Axes of the slice: x: 2, y: 2, z: 4, core: 2. Of those that a mesh axis runs over, the one named last changes fastest.
Arguments:
- images: bfloat16 [4096, 4096], P(('img', 'ref')), may hold values from -6 to 6
- exponents: int32 [4096], P('img'), may hold values from 0 to 8
- references: bfloat16 [6144, 4096], P('ref'), may hold values from -8 to 8
- partners: int32 [6144], P('ref'), may hold values from 0 to 6143, as said below
Outputs:
- symmetric_sums: float32 [6144, 4096], P('ref', 'img')
The draws below stay inside these ranges and needn't reach their ends.
Inputs may be any that keep to these rules, and one draw needn't show every extreme that they name: partners is an involution without fixed points; partners[r] lies in the block of 768 references that starts 6144 / 2 references after or before the start of r's block.
All inputs are finite; a program needn't handle non-finite values.
Results may differ from the reference program's by a relative error of at most 0.0033.
Values may be sent and summed in bfloat16 or wider, within the bound.
No kernel may reach another device: no remote copies, remote signals or barrier semaphores. Data moves between devices by JAX's collectives and lax.ppermute only.
A program may use at most 64 MiB of HBM per device.

```python
import jax
import jax.numpy as jnp
from jax import lax

K = 4096
REF_DEV = 768
NREF = 6144
NIMG = 4096


def draw_references(key, part):
    scale_key = jax.random.fold_in(key, 11)
    value_key = jax.random.fold_in(key, 12)
    scales = jnp.exp(jax.random.uniform(scale_key, (NREF, 1), jnp.float32, jnp.log(0.5), jnp.log(1.5)))
    values = jnp.clip(jax.random.normal(value_key, (NREF, K), jnp.float32), -5.0, 5.0)
    return (values * scales).astype(jnp.bfloat16)


def draw_partners(key, part):
    pair_count = NREF // REF_DEV // 2
    keys = jax.random.split(jax.random.fold_in(key, 21), pair_count)
    perms = jax.vmap(lambda k: jax.random.permutation(k, REF_DEV))(keys).astype(jnp.int32)
    lower = jnp.arange(NREF // 2, dtype=jnp.int32)
    blocks = lower // REF_DEV
    local = lower % REF_DEV
    upper = (NREF // 2 + blocks * REF_DEV + perms[blocks, local]).astype(jnp.int32)
    result = jnp.zeros((NREF,), jnp.int32)
    result = result.at[lower].set(upper)
    result = result.at[upper].set(lower)
    return result


def with_ends(drawn, rng, smallest, high):
    longest = drawn.shape.index(max(drawn.shape))
    spots = []
    for shift in (0, 1):
        where = [jax.random.randint(jax.random.fold_in(rng, axis), (), 0, length) for axis, length in enumerate(drawn.shape)]
        where[longest] = (where[longest] + shift) % drawn.shape[longest]
        spots.append(tuple(where))
    return drawn.at[spots[0]].set(smallest).at[spots[1]].set(high)


def block_scale(key, shape, cuts, smallest, top_value):
    loudness = 1.0
    for axis_at, blocks in cuts:
        steps = jax.random.uniform(jax.random.fold_in(jax.random.fold_in(key, 6), axis_at), (blocks,), jnp.float32, smallest / len(cuts), top_value / len(cuts))
        loudness = loudness * jnp.repeat(jnp.exp(steps), shape[axis_at] // blocks).reshape((-1,) + (1,) * (len(shape) - 1 - axis_at))
    return loudness


def noise(own_key, shape, spread, bound, pieces=(), kind=jnp.bfloat16):
    factor_of = block_scale(own_key, shape, pieces, -0.22, 0.18) if pieces else 1.0
    array = jax.random.normal(own_key, shape, jnp.float32) * spread * factor_of
    return jnp.minimum(jnp.maximum(array, -bound), bound).astype(kind)


def setup_inputs(seed: int = 0) -> dict:
    streams_of = jax.random.split(jax.random.key(seed), 5)
    return {
        "images": noise(streams_of[0], (NIMG, K), 1.0, 6.0, ((0, 32),)),
        "exponents": with_ends(jax.random.randint(streams_of[1], (NIMG,), 0, 9), jax.random.fold_in(streams_of[1], 1), 0, 8).astype(jnp.int32),
        "references": draw_references(jax.random.fold_in(streams_of[4], 71), 0),
        "partners": draw_partners(jax.random.fold_in(streams_of[4], 71), 0),
    }


def reference(images, exponents, references, partners):
    width = references.shape[1]
    norms = lax.optimization_barrier(jnp.sum(jnp.square(references.astype(jnp.float32)), axis=1)) / width
    block = min(512, NIMG)
    count = NIMG // block
    image_blocks = images.reshape(count, block, width)
    expo_blocks = exponents.reshape(count, block)

    def accumulate(total, pair):
        rows, expo = pair
        scores = jnp.dot(rows, references.T, preferred_element_type=jnp.float32) / jnp.sqrt(jnp.float32(width))
        scores = scores - 0.5 * norms[None, :] - 0.25 * expo.astype(jnp.float32)[:, None]
        weights = jnp.exp(scores).astype(jnp.bfloat16)
        return (total + jnp.dot(weights.T, rows, preferred_element_type=jnp.float32), None)
    start = jnp.zeros((references.shape[0], width), jnp.float32)
    sums, _ = lax.scan(accumulate, start, (image_blocks, expo_blocks))
    partner_rows = jnp.take(sums, partners.astype(jnp.int32), axis=0)
    return 0.5 * (sums + partner_rows) / jnp.sqrt(jnp.float32(NIMG))
```

```python
import jax
import jax.numpy as jnp
from jax import lax
from jax.sharding import PartitionSpec as P

F32 = jnp.float32
BF16 = jnp.bfloat16
ROW_CHUNKS = 2


def swap(block, axis, bit):
    count = lax.axis_size(axis)
    return lax.ppermute(block, axis, [(i, i ^ bit) for i in range(count)])


def gather_pieces(images, count):
    pieces = [None] * count
    pieces[0] = images
    for k in range(2, count, 2):
        low = k & -k
        pieces[k] = swap(pieces[k ^ low], "ref", low)
    for k in range(0, count, 2):
        pieces[k + 1] = swap(pieces[k], "ref", 1)
    return pieces


def line_sum(parts, axis):
    n = lax.axis_size(axis)
    me = lax.axis_index(axis)
    width = parts[0].shape[1] // n

    def block(part, d):
        return lax.dynamic_slice_in_dim(part, jnp.clip(d, 0, n - 1) * width, width, axis=1)

    right = [None] * len(parts)
    left = [None] * len(parts)
    for step in range(1, n):
        up = [(z, z + 1) for z in range(n - 1) if z <= step - 1]
        down = [(n - 1 - a, n - 1 - b) for a, b in up]
        for c, part in enumerate(parts):
            r = block(part, n + me - step)
            l = block(part, me - n + step)
            if step > 1:
                r = r + right[c].astype(F32)
                l = l + left[c].astype(F32)
            right[c] = lax.ppermute(r.astype(BF16), axis, up)
            left[c] = lax.ppermute(l.astype(BF16), axis, down)
    return [
        block(part, me) + right[c].astype(F32) + left[c].astype(F32)
        for c, part in enumerate(parts)
    ]


def body(images, exponents, references, partners):
    rows, width = references.shape
    half = rows // 2
    count = lax.axis_size("ref")
    me = lax.axis_index("ref")
    img_rows = images.shape[0]
    total_images = img_rows * count * lax.axis_size("img")
    top = count // 2
    upper = me // top

    pieces = gather_pieces(images, count)

    own_order = jnp.arange(rows, dtype=jnp.int32)
    place = jnp.where(upper == 0, own_order, partners % rows)
    place = (place + upper * half) % rows
    one_hot = (own_order[:, None] == place[None, :]).astype(BF16)
    refs = jnp.dot(one_hot, references, preferred_element_type=F32).astype(BF16)
    norms = jnp.sum(jnp.square(refs.astype(F32)), axis=1) / width
    inv_root = 1.0 / jnp.sqrt(F32(width))
    offsets = exponents.reshape(count, img_rows)[me ^ jnp.arange(count)].astype(F32) * 0.25

    apart = top // 2
    blocks, weights = [], []
    for m in range(count // 2):
        block = jnp.concatenate([pieces[2 * m], pieces[2 * m + 1]], axis=0)
        scores = lax.dot_general(refs, block, (((1,), (1,)), ((), ())), preferred_element_type=F32) * inv_root
        scores = scores - 0.5 * norms[:, None] - offsets[2 * m : 2 * m + 2].reshape(1, 2 * img_rows)
        blocks.append(block)
        weights.append(jnp.exp(scores).astype(BF16))
    means = [None] * len(weights)
    for m, w in enumerate(weights):
        other = swap(w[half:], "ref", top)
        at = m ^ apart
        means[at] = (0.5 * weights[at][:half].astype(F32) + 0.5 * other.astype(F32)).astype(BF16)
    last = [m for m in range(count // 2) if m | apart == count // 2 - 1]
    first = [m for m in range(count // 2) if m not in last]

    def joined(arrays, which, axis):
        return jnp.concatenate([arrays[m] for m in which], axis=axis)

    scale = 1.0 / jnp.sqrt(F32(total_images))
    parts = []
    chunk = half // ROW_CHUNKS
    early = jnp.dot(joined(means, first, 1), joined(blocks, first, 0), preferred_element_type=F32)
    late_means, late_blocks = joined(means, last, 1), joined(blocks, last, 0)
    for c in range(ROW_CHUNKS):
        at = slice(c * chunk, (c + 1) * chunk)
        late = jnp.dot(late_means[at], late_blocks, preferred_element_type=F32)
        parts.append((early[at] + late) * scale)
    done = line_sum(parts, "img")
    other = [swap(part.astype(BF16), "ref", top).astype(F32) for part in done]
    return jnp.take(jnp.concatenate(done + other, axis=0), place, axis=0)


def solution(mesh):
    in_specs = (P(("img", "ref"), None), P("img"), P("ref", None), P("ref"))
    out_specs = P("ref", "img")
    return jax.shard_map(body, mesh=mesh, in_specs=in_specs, out_specs=out_specs, check_vma=False)
```

```python
import jax
import jax.numpy as jnp
from jax import lax
from jax.sharding import PartitionSpec as P

F32 = jnp.float32
BF16 = jnp.bfloat16
ROW_CHUNKS = 3


def swap(block, axis, bit):
    count = lax.axis_size(axis)
    return lax.ppermute(block, axis, [(i, i ^ bit) for i in range(count)])


def after(array, *others):
    return lax.optimization_barrier((array, *others))[0]


def halving_sum(part, axis, bit):
    n = lax.axis_size(axis)
    side = lax.axis_index(axis) // bit % 2
    blocks = n // bit
    width = part.shape[1] // blocks

    def of_side(s):
        cut = [lax.dynamic_slice_in_dim(part, (2 * j + s) * width, width, axis=1) for j in range(blocks // 2)]
        return jnp.concatenate(cut, axis=1)

    return of_side(side) + swap(of_side(1 - side).astype(BF16), axis, bit).astype(F32)


def body(images, exponents, references, partners):
    rows, width = references.shape
    half = rows // 2
    count = lax.axis_size("ref")
    me = lax.axis_index("ref")
    img_rows = images.shape[0]
    total_images = img_rows * count * lax.axis_size("img")
    top = count // 2
    upper = me // top

    pieces = {0: images}
    for k in reversed(range(2, count, 2)):
        if k & (k - 1) == 0:
            pieces[k] = swap(images, "ref", k)
    pieces[1] = swap(images, "ref", 1)

    own_order = jnp.arange(rows, dtype=jnp.int32)
    place = jnp.where(upper == 0, own_order, partners % rows)
    place = (place + upper * half) % rows
    one_hot = (own_order[:, None] == place[None, :]).astype(BF16)
    refs = jnp.dot(one_hot, references, preferred_element_type=F32).astype(BF16)
    norms = jnp.sum(jnp.square(refs.astype(F32)), axis=1) / width
    inv_root = 1.0 / jnp.sqrt(F32(width))
    offsets = exponents.reshape(count, img_rows)[me ^ jnp.arange(count)].astype(F32) * 0.25

    apart = top // 2
    blocks, weights = [], []

    def add_block(m):
        block = jnp.concatenate([pieces[2 * m], pieces[2 * m + 1]], axis=0)
        scores = lax.dot_general(refs, block, (((1,), (1,)), ((), ())), preferred_element_type=F32) * inv_root
        scores = scores - 0.5 * norms[:, None] - offsets[2 * m : 2 * m + 2].reshape(1, 2 * img_rows)
        blocks.append(block)
        weights.append(jnp.exp(scores).astype(BF16))

    add_block(0)
    for k in range(2, count, 2):
        low = k & -k
        if low == k:
            pieces[k] = after(pieces[k], weights[0])
        else:
            pieces[k] = swap(pieces[k ^ low], "ref", low)
        pieces[k + 1] = swap(pieces[k], "ref", 1)
    for m in range(1, count // 2):
        add_block(m)
    means = [None] * len(weights)
    for m, w in enumerate(weights):
        other = swap(w[half:], "ref", top)
        at = m ^ apart
        means[at] = (0.5 * weights[at][:half].astype(F32) + 0.5 * other.astype(F32)).astype(BF16)
    last = [m for m in range(count // 2) if m | apart == count // 2 - 1]
    first = [m for m in range(count // 2) if m not in last]

    def joined(arrays, which, axis):
        return jnp.concatenate([arrays[m] for m in which], axis=axis)

    scale = 1.0 / jnp.sqrt(F32(total_images))
    parts = []
    chunk = half // ROW_CHUNKS
    early = jnp.dot(joined(means, first, 1), joined(blocks, first, 0), preferred_element_type=F32)
    late_means, late_blocks = joined(means, last, 1), joined(blocks, last, 0)
    for c in range(ROW_CHUNKS):
        at = slice(c * chunk, (c + 1) * chunk)
        late = jnp.dot(late_means[at], late_blocks, preferred_element_type=F32)
        parts.append((early[at] + late) * scale)
    bit = 1
    while bit < lax.axis_size("img"):
        parts = [halving_sum(part, "img", bit) for part in parts]
        bit *= 2
    other = [swap(part.astype(BF16), "ref", top).astype(F32) for part in parts]
    return jnp.concatenate(parts + other, axis=0).at[place].get(mode="promise_in_bounds")


def solution(mesh):
    in_specs = (P(("img", "ref"), None), P("img"), P("ref", None), P("ref"))
    out_specs = P("ref", "img")
    return jax.shard_map(body, mesh=mesh, in_specs=in_specs, out_specs=out_specs, check_vma=False)
```

```python
import jax
import jax.numpy as jnp
from jax import lax
from jax.sharding import PartitionSpec as P

F32 = jnp.float32
BF16 = jnp.bfloat16
HALVED = 2
ROW_CHUNKS = 2


def swap(block, axis, bit):
    count = lax.axis_size(axis)
    return lax.ppermute(block, axis, [(i, i ^ bit) for i in range(count)])


def after(array, *others):
    return lax.optimization_barrier((array, *others))[0]


def halving_sum(part, axis, bit):
    n = lax.axis_size(axis)
    side = lax.axis_index(axis) // bit % 2
    blocks = n // bit
    width = part.shape[1] // blocks

    def of_side(s):
        cut = [lax.dynamic_slice_in_dim(part, (2 * j + s) * width, width, axis=1) for j in range(blocks // 2)]
        return jnp.concatenate(cut, axis=1)

    return of_side(side) + swap(of_side(1 - side).astype(BF16), axis, bit).astype(F32)


def body(images, exponents, references, partners):
    rows, width = references.shape
    half = rows // 2
    count = lax.axis_size("ref")
    me = lax.axis_index("ref")
    planes = lax.axis_size("img")
    plane = lax.axis_index("img")
    img_rows = images.shape[0]
    total_images = img_rows * count * planes
    top = count // 2
    upper = me // top
    apart = top // 2
    columns = width // planes

    pieces = {0: images}
    for k in reversed(range(2, count, 2)):
        if k & (k - 1) == 0:
            pieces[k] = swap(images, "ref", k)
    pieces[1] = swap(images, "ref", 1)

    def of_plane(array, z):
        return lax.dynamic_slice_in_dim(array, z * columns, columns, axis=1)

    far = {0: jnp.concatenate([swap(of_plane(images, plane ^ r), "img", r) for r in range(1, planes)], axis=0)}

    kept = half * HALVED // 4
    both = half - kept
    own_order = jnp.arange(rows, dtype=jnp.int32)
    pair = partners % rows
    mirrored = jnp.where(
        pair < half,
        jnp.where(pair < kept, pair + half + both, pair + both),
        jnp.where(pair < half + both, pair - both, pair - half - both),
    )
    place = jnp.where(upper == 0, own_order, mirrored)
    one_hot = (own_order[:, None] == place[None, :]).astype(BF16)
    refs = jnp.dot(one_hot, references, preferred_element_type=F32).astype(BF16)
    norms = jnp.sum(jnp.square(refs.astype(F32)), axis=1) / width
    inv_root = 1.0 / jnp.sqrt(F32(width))
    offsets = exponents.reshape(count, img_rows)[me ^ jnp.arange(count)].astype(F32) * 0.25
    scale = 1.0 / jnp.sqrt(F32(total_images))

    weights, sent = {}, {}

    def add_block(m):
        block = jnp.concatenate([pieces[2 * m], pieces[2 * m + 1]], axis=0)
        scores = lax.dot_general(refs, block, (((1,), (1,)), ((), ())), preferred_element_type=F32) * inv_root
        scores = scores - 0.5 * norms[:, None] - offsets[2 * m : 2 * m + 2].reshape(1, 2 * img_rows)
        weights[m] = jnp.exp(scores).astype(BF16)
        start = half + both if m < apart else kept
        sent[m ^ apart] = swap(weights[m][start:], "ref", top)

    def mean(a, b):
        return (0.5 * a.astype(F32) + 0.5 * b.astype(F32)).astype(BF16)

    def kept_sums(ms, at):
        w = [mean(weights[m][:kept], sent[m][-kept:])[at] for m in ms]
        x = [pieces[k] for m in ms for k in (2 * m, 2 * m + 1)]
        return jnp.dot(jnp.concatenate(w, axis=1), jnp.concatenate(x, axis=0), preferred_element_type=F32)

    def gathered_weights(m):
        theirs = jnp.concatenate([sent[m][both : 2 * both], sent[m][:both]], axis=0)
        every = lax.all_gather(mean(weights[m][kept : half + both], theirs), "img", axis=0)
        by_plane = [lax.dynamic_index_in_dim(every, plane ^ r, 0, keepdims=False) for r in range(planes)]
        return jnp.concatenate(by_plane, axis=1)

    def both_sums(ms):
        w = jnp.concatenate([gathered_weights(m) for m in ms], axis=1)
        x = []
        for m in ms:
            for r in range(planes):
                for k in (2 * m, 2 * m + 1):
                    rest = far[k][(r - 1) * img_rows : r * img_rows]
                    x.append(of_plane(pieces[k], plane) if r == 0 else rest)
        return jnp.dot(w, jnp.concatenate(x, axis=0), preferred_element_type=F32)

    add_block(0)
    blocks = count // 2
    last = [m for m in range(blocks) if m | apart == blocks - 1]
    first = [m for m in range(blocks) if m not in last]
    for m in range(1, blocks):
        k = 2 * m
        low = k & -k
        if low == k:
            pieces[k] = after(pieces[k], weights[0])
        else:
            pieces[k] = swap(pieces[k ^ low], "ref", low)
        if m == blocks - 1:
            early = kept_sums(first, slice(None))
            pieces[k] = after(pieces[k], early)
        pieces[k + 1] = swap(pieces[k], "ref", 1)
        if m == blocks - 1:
            far[0] = after(far[0], pieces[k])
            for f in range(2, top, 2):
                far[f] = swap(far[f ^ (f & -f)], "ref", f & -f)
            for f in range(0, top, 2):
                far[f + 1] = swap(far[f], "ref", 1)
        add_block(m)

    parts = []
    chunk = kept // ROW_CHUNKS
    for c in range(ROW_CHUNKS):
        at = slice(c * chunk, (c + 1) * chunk)
        parts.append((early[at] + kept_sums(last, at)) * scale)
    bit = 1
    while bit < planes:
        parts = [halving_sum(part, "img", bit) for part in parts]
        bit *= 2
    shared = both_sums(range(apart)) * scale
    theirs = swap(shared.astype(BF16), "ref", top).astype(F32)
    shared = shared + jnp.concatenate([theirs[both:], theirs[:both]], axis=0)
    other = [swap(part.astype(BF16), "ref", top).astype(F32) for part in parts]
    return jnp.concatenate(parts + [shared] + other, axis=0).at[place].get(mode="promise_in_bounds")


def solution(mesh):
    in_specs = (P(("img", "ref"), None), P("img"), P("ref", None), P("ref"))
    out_specs = P("ref", "img")
    return jax.shard_map(body, mesh=mesh, in_specs=in_specs, out_specs=out_specs, check_vma=False)
```

```python
import jax
import jax.numpy as jnp
from jax import lax
from jax.sharding import PartitionSpec as P

F32 = jnp.float32
BF16 = jnp.bfloat16
HALVED = 4
ROW_CHUNKS = 2


def swap(block, axis, bit):
    count = lax.axis_size(axis)
    return lax.ppermute(block, axis, [(i, i ^ bit) for i in range(count)])


def after(array, *others):
    return lax.optimization_barrier((array, *others))[0]


def halving_sum(part, axis, bit):
    n = lax.axis_size(axis)
    side = lax.axis_index(axis) // bit % 2
    blocks = n // bit
    width = part.shape[1] // blocks

    def of_side(s):
        cut = [lax.dynamic_slice_in_dim(part, (2 * j + s) * width, width, axis=1) for j in range(blocks // 2)]
        return jnp.concatenate(cut, axis=1)

    return of_side(side) + swap(of_side(1 - side).astype(BF16), axis, bit).astype(F32)


def gather_ends(block, axis):
    return jnp.stack([block, swap(block, axis, 1)])


def gather_middle(two, axis):
    return lax.ppermute(two[::-1], axis, [(1, 2), (2, 1)])


def gather_out(four, axis):
    me = lax.axis_index(axis)
    out = lax.ppermute(four[::-1], axis, [(1, 0), (2, 3)])
    return jnp.where((me == 1) | (me == 2), four, out)


def gather_any(block, axis):
    every = lax.all_gather(block, axis, axis=0)
    return [lax.dynamic_index_in_dim(every, lax.axis_index(axis) ^ r, 0, keepdims=False) for r in range(lax.axis_size(axis))]


def body(images, exponents, references, partners):
    rows, width = references.shape
    half = rows // 2
    count = lax.axis_size("ref")
    me = lax.axis_index("ref")
    planes = lax.axis_size("img")
    plane = lax.axis_index("img")
    img_rows = images.shape[0]
    total_images = img_rows * count * planes
    top = count // 2
    upper = me // top
    apart = top // 2
    columns = width // planes

    pieces = {0: images}
    for k in reversed(range(2, count, 2)):
        if k & (k - 1) == 0:
            pieces[k] = swap(images, "ref", k)
    pieces[1] = swap(images, "ref", 1)

    def of_plane(array, z):
        return lax.dynamic_slice_in_dim(array, z * columns, columns, axis=1)

    far = {0: jnp.concatenate([swap(of_plane(images, plane ^ r), "img", r) for r in range(1, planes)], axis=0)}

    kept = half * HALVED // 6
    both = half - kept
    own_order = jnp.arange(rows, dtype=jnp.int32)
    pair = partners % rows
    mirrored = jnp.where(
        pair < half,
        jnp.where(pair < kept, pair + half + both, pair + both),
        jnp.where(pair < half + both, pair - both, pair - half - both),
    )
    place = jnp.where(upper == 0, own_order, mirrored)
    one_hot = (own_order[:, None] == place[None, :]).astype(BF16)
    refs = jnp.dot(one_hot, references, preferred_element_type=F32).astype(BF16)
    norms = jnp.sum(jnp.square(refs.astype(F32)), axis=1) / width
    inv_root = 1.0 / jnp.sqrt(F32(width))
    offsets = exponents.reshape(count, img_rows)[me ^ jnp.arange(count)].astype(F32) * 0.25
    scale = 1.0 / jnp.sqrt(F32(total_images))

    weights, sent = {}, {}

    def add_block(m):
        block = jnp.concatenate([pieces[2 * m], pieces[2 * m + 1]], axis=0)
        scores = lax.dot_general(refs, block, (((1,), (1,)), ((), ())), preferred_element_type=F32) * inv_root
        scores = scores - 0.5 * norms[:, None] - offsets[2 * m : 2 * m + 2].reshape(1, 2 * img_rows)
        weights[m] = jnp.exp(scores).astype(BF16)
        start = half + both if m < apart else kept
        sent[m ^ apart] = swap(weights[m][start:], "ref", top)

    def mean(a, b):
        return (0.5 * a.astype(F32) + 0.5 * b.astype(F32)).astype(BF16)

    def kept_sums(ms, at):
        w = [mean(weights[m][:kept], sent[m][-kept:])[at] for m in ms]
        x = [pieces[k] for m in ms for k in (2 * m, 2 * m + 1)]
        return jnp.dot(jnp.concatenate(w, axis=1), jnp.concatenate(x, axis=0), preferred_element_type=F32)

    def both_weights(m):
        theirs = jnp.concatenate([sent[m][both : 2 * both], sent[m][:both]], axis=0)
        return mean(weights[m][kept : half + both], theirs)

    def both_sums(m, w):
        even, odd = 2 * m, 2 * m + 1
        ws = [w[0]] + [a[:, :img_rows] for a in w[1:]] + [a[:, img_rows:] for a in w[1:]]
        xs = [of_plane(pieces[even], plane), of_plane(pieces[odd], plane), far[even], far[odd]]
        return jnp.dot(jnp.concatenate(ws, axis=1), jnp.concatenate(xs, axis=0), preferred_element_type=F32)

    blocks = count // 2
    last = [m for m in range(blocks) if m | apart == blocks - 1]
    first = [m for m in range(blocks) if m not in last]
    early_both = [m for m in first if m < apart]
    late_both = [m for m in last if m < apart]
    line = planes == 4

    add_block(0)
    for m in reversed(range(1, blocks)):
        if m & (m - 1) == 0:
            pieces[2 * m] = after(pieces[2 * m], weights[0])
            if m == 1:
                pieces[2 * m] = after(pieces[2 * m], far[0])
            pieces[2 * m + 1] = swap(pieces[2 * m], "ref", 1)
    for m in range(1, blocks - 1):
        k = 2 * m
        if m & (m - 1):
            pieces[k] = swap(pieces[k ^ (k & -k)], "ref", k & -k)
            pieces[k + 1] = swap(pieces[k], "ref", 1)
    k = count - 2
    pieces[k] = swap(pieces[k ^ 2], "ref", 2)
    for m in sorted(range(1, blocks - 1), reverse=True):
        add_block(m)
    early = kept_sums(first, slice(None))
    steps = {m: gather_ends(both_weights(m), "img") for m in early_both} if line else {}
    pieces[k] = after(pieces[k], early, *steps.values())
    pieces[k + 1] = swap(pieces[k], "ref", 1)
    far[0] = after(far[0], pieces[k])
    for f in range(2, top, 2):
        far[f] = swap(far[f ^ (f & -f)], "ref", f & -f)
    for f in range(0, top, 2):
        far[f + 1] = swap(far[f], "ref", 1)
    add_block(blocks - 1)

    if line:
        rest = {m: gather_middle(steps[m], "img") for m in early_both}
        for m in early_both:
            sent[blocks - 1 ^ apart] = after(sent[blocks - 1 ^ apart], rest[m])
        rest = {m: gather_out(rest[m], "img") for m in early_both}
        for m in late_both:
            steps[m] = gather_ends(both_weights(m), "img")
            rest[m] = gather_out(gather_middle(steps[m], "img"), "img")
        gathered = {m: [steps[m][0], steps[m][1], rest[m][0], rest[m][1]] for m in range(apart)}
    else:
        gathered = {m: gather_any(both_weights(m), "img") for m in range(apart)}

    parts = []
    chunk = kept // ROW_CHUNKS
    for c in range(ROW_CHUNKS):
        at = slice(c * chunk, (c + 1) * chunk)
        parts.append((early[at] + kept_sums(last, at)) * scale)
    bit = 1
    while bit < planes:
        parts = [halving_sum(part, "img", bit) for part in parts]
        bit *= 2
    shared = sum(both_sums(m, gathered[m]) for m in range(apart)) * scale
    theirs = swap(shared.astype(BF16), "ref", top).astype(F32)
    shared = shared + jnp.concatenate([theirs[both:], theirs[:both]], axis=0)
    other = [swap(part.astype(BF16), "ref", top).astype(F32) for part in parts]
    return jnp.concatenate(parts + [shared] + other, axis=0).at[place].get(mode="promise_in_bounds")


def solution(mesh):
    in_specs = (P(("img", "ref"), None), P("img"), P("ref", None), P("ref"))
    out_specs = P("ref", "img")
    return jax.shard_map(body, mesh=mesh, in_specs=in_specs, out_specs=out_specs, check_vma=False)
```

```python
import jax
import jax.numpy as jnp
from jax import lax
from jax.sharding import PartitionSpec as P

F32 = jnp.float32
BF16 = jnp.bfloat16
HALVED = 3
ROW_CHUNKS = 2


def swap(block, axis, bit):
    count = lax.axis_size(axis)
    return lax.ppermute(block, axis, [(i, i ^ bit) for i in range(count)])


def after(array, *others):
    return lax.optimization_barrier((array, *others))[0]


def halving_sum(part, axis, bit):
    n = lax.axis_size(axis)
    side = lax.axis_index(axis) // bit % 2
    blocks = n // bit
    width = part.shape[1] // blocks

    def of_side(s):
        cut = [lax.dynamic_slice_in_dim(part, (2 * j + s) * width, width, axis=1) for j in range(blocks // 2)]
        return jnp.concatenate(cut, axis=1)

    return of_side(side) + swap(of_side(1 - side).astype(BF16), axis, bit).astype(F32)


def gather_ends(block, axis):
    return jnp.concatenate([block, swap(block, axis, 1)], axis=1)


def gather_middle(two, axis):
    return lax.ppermute(two, axis, [(1, 2), (2, 1)])


def gather_out(four, axis):
    return lax.ppermute(four, axis, [(1, 0), (2, 3)])


def gather_rest(four, out, axis):
    me = lax.axis_index(axis)
    half = four.shape[1] // 2
    turned = jnp.concatenate([four[:, half:], four[:, :half]], axis=1)
    return jnp.where((me == 1) | (me == 2), turned, out)


def gather_any(block, axis):
    every = lax.all_gather(block, axis, axis=0)
    n, me = lax.axis_size(axis), lax.axis_index(axis)
    return jnp.concatenate([lax.dynamic_index_in_dim(every, me ^ r, 0, keepdims=False) for r in range(n)], axis=1)


def body(images, exponents, references, partners):
    rows, width = references.shape
    half = rows // 2
    count = lax.axis_size("ref")
    me = lax.axis_index("ref")
    planes = lax.axis_size("img")
    plane = lax.axis_index("img")
    img_rows = images.shape[0]
    total_images = img_rows * count * planes
    top = count // 2
    upper = me // top
    apart = top // 2
    columns = width // planes

    pieces = {0: images}
    for k in reversed(range(2, count, 2)):
        if k & (k - 1) == 0:
            pieces[k] = swap(images, "ref", k)
    pieces[1] = swap(images, "ref", 1)

    def of_plane(array, z):
        return lax.dynamic_slice_in_dim(array, z * columns, columns, axis=1)

    quarters = [swap(of_plane(images, plane ^ r), "img", r) for r in range(1, planes)]
    far = {}

    kept = half * HALVED // 6
    both = half - kept
    own_order = jnp.arange(rows, dtype=jnp.int32)
    pair = partners % rows
    mirrored = jnp.where(
        pair < half,
        jnp.where(pair < kept, pair + half + both, pair + both),
        jnp.where(pair < half + both, pair - both, pair - half - both),
    )
    place = jnp.where(upper == 0, own_order, mirrored)
    one_hot = (own_order[:, None] == place[None, :]).astype(BF16)
    refs = jnp.dot(one_hot, references, preferred_element_type=F32).astype(BF16)
    norms = jnp.sum(jnp.square(refs.astype(F32)), axis=1) / width
    inv_root = 1.0 / jnp.sqrt(F32(width))
    offsets = exponents.reshape(count, img_rows)[me ^ jnp.arange(count)].astype(F32) * 0.25
    scale = 1.0 / jnp.sqrt(F32(total_images))

    weights, sent = {}, {}

    def score(m):
        block = jnp.concatenate([pieces[2 * m], pieces[2 * m + 1]], axis=0)
        scores = lax.dot_general(refs, block, (((1,), (1,)), ((), ())), preferred_element_type=F32) * inv_root
        scores = scores - 0.5 * norms[:, None] - offsets[2 * m : 2 * m + 2].reshape(1, 2 * img_rows)
        weights[m] = jnp.exp(scores).astype(BF16)

    def send(m):
        start = half + both if m < apart else kept
        sent[m ^ apart] = swap(weights[m][start:], "ref", top)

    def mean(a, b):
        return (0.5 * a.astype(F32) + 0.5 * b.astype(F32)).astype(BF16)

    def kept_sums(ms, at):
        w = [mean(weights[m][:kept], sent[m][-kept:])[at] for m in ms]
        x = [pieces[k] for m in ms for k in (2 * m, 2 * m + 1)]
        return jnp.dot(jnp.concatenate(w, axis=1), jnp.concatenate(x, axis=0), preferred_element_type=F32)

    def both_weights(m):
        theirs = jnp.concatenate([sent[m][both : 2 * both], sent[m][:both]], axis=0)
        return mean(weights[m][kept : half + both], theirs)

    def both_sums(m, w):
        xs = [of_plane(pieces[2 * m], plane), of_plane(pieces[2 * m + 1], plane)]
        for r in range(planes - 1):
            xs += [far[k][r * img_rows : (r + 1) * img_rows] for k in (2 * m, 2 * m + 1)]
        return jnp.dot(w, jnp.concatenate(xs, axis=0), preferred_element_type=F32)

    blocks = count // 2
    last = [m for m in range(blocks) if m | apart == blocks - 1]
    first = [m for m in range(blocks) if m not in last]
    early_both = [m for m in first if m < apart]
    late_both = [m for m in last if m < apart]
    line = planes == 4
    end = blocks - 1

    score(0)
    send(0)
    singles = [m for m in reversed(range(1, blocks)) if m & (m - 1) == 0]
    before = weights[0]
    for m in singles:
        pieces[2 * m] = after(pieces[2 * m], before)
        pieces[2 * m + 1] = swap(pieces[2 * m], "ref", 1)
        before = pieces[2 * m]
    for m in range(1, blocks):
        if m & (m - 1):
            k = 2 * m
            pieces[k] = swap(pieces[k ^ (k & -k)], "ref", k & -k)
            if m != end:
                pieces[k + 1] = swap(pieces[k], "ref", 1)
    for m in sorted(range(1, end), reverse=True):
        if m == 1:
            tied = lax.optimization_barrier((pieces[2], weights[apart], sent[apart], *quarters))
            pieces[2], weights[apart], sent[apart] = tied[:3]
            far[0] = jnp.concatenate(tied[3:], axis=0)
        score(m)
        send(m)
    starts = {m: both_weights(m) for m in early_both}
    ends = {m: gather_ends(starts[m], "img") for m in early_both} if line else {}
    early = kept_sums(first, slice(None))
    pieces[2 * end], far[0], early, *tied = lax.optimization_barrier((pieces[2 * end], far[0], early, *ends.values()))
    ends = dict(zip(ends, tied))
    pieces[2 * end + 1] = swap(pieces[2 * end], "ref", 1)
    for f in range(2, top, 2):
        far[f] = swap(far[f ^ (f & -f)], "ref", f & -f)
    middles = {m: gather_middle(ends[m], "img") for m in ends}
    score(end)
    send(end)
    at = end ^ apart
    weights[end], *tied = lax.optimization_barrier((weights[end], *middles.values()))
    middles = dict(zip(middles, tied))
    sent[at], *tied = lax.optimization_barrier((sent[at], *middles.values()))
    middles = dict(zip(middles, tied))
    outs = {m: gather_out(middles[m], "img") for m in middles}
    late = {m: both_weights(m) for m in late_both}
    late_ends = {m: gather_ends(late[m], "img") for m in late_both} if line else {}

    parts = []
    chunk = kept // ROW_CHUNKS
    for c in range(ROW_CHUNKS):
        at = slice(c * chunk, (c + 1) * chunk)
        parts.append((early[at] + kept_sums(last, at)) * scale)
    if line:
        parts, ties = lax.optimization_barrier((parts, (late_ends, far, outs)))
        late_ends, far, outs = ties
        late_middles = {m: gather_middle(late_ends[m], "img") for m in late_both}
    for f in range(0, top, 2):
        far[f + 1] = swap(far[f], "ref", 1)
    parts = [halving_sum(part, "img", 1) for part in parts]
    if line:
        parts[0], late_middles = lax.optimization_barrier((parts[0], late_middles))
        late_outs = {m: gather_out(late_middles[m], "img") for m in late_both}
    bit = 2
    while bit < planes:
        parts = [halving_sum(part, "img", bit) for part in parts]
        bit *= 2
    if line:
        ends.update(late_ends)
        middles.update(late_middles)
        outs.update(late_outs)
        gathered = {m: jnp.concatenate([ends[m], gather_rest(middles[m], outs[m], "img")], axis=1) for m in ends}
    else:
        gathered = {m: gather_any(both_weights(m), "img") for m in range(apart)}
    shared = sum(both_sums(m, gathered[m]) for m in range(apart)) * scale
    theirs = swap(shared.astype(BF16), "ref", top).astype(F32)
    shared = shared + jnp.concatenate([theirs[both:], theirs[:both]], axis=0)
    other = [swap(part.astype(BF16), "ref", top).astype(F32) for part in parts]
    return jnp.concatenate(parts + [shared] + other, axis=0).at[place].get(mode="promise_in_bounds")


def solution(mesh):
    in_specs = (P(("img", "ref"), None), P("img"), P("ref", None), P("ref"))
    out_specs = P("ref", "img")
    return jax.shard_map(body, mesh=mesh, in_specs=in_specs, out_specs=out_specs, check_vma=False)
```

```python
import functools
import math

import jax
import jax.numpy as jnp
from jax import lax
from jax.experimental import pallas as pl
from jax.experimental.pallas import tpu as pltpu
from jax.sharding import PartitionSpec as P

F32 = jnp.float32
BF16 = jnp.bfloat16
HALVED = 3
ROW_CHUNKS = 2
SCORE_ROWS = 256
SCORE_COST = 1000


def swap(block, axis, bit):
    count = lax.axis_size(axis)
    return lax.ppermute(block, axis, [(i, i ^ bit) for i in range(count)])


def after(array, *others):
    return lax.optimization_barrier((array, *others))[0]


def halves(part, axis, bit):
    n = lax.axis_size(axis)
    side = lax.axis_index(axis) // bit % 2
    blocks = n // bit
    width = part.shape[1] // blocks

    def of_side(s):
        cut = [lax.dynamic_slice_in_dim(part, (2 * j + s) * width, width, axis=1) for j in range(blocks // 2)]
        return jnp.concatenate(cut, axis=1)

    return of_side(side), of_side(1 - side).astype(BF16)


def gather_ends(block, axis):
    return jnp.concatenate([block, swap(block, axis, 1)], axis=1)


def gather_middle(two, axis):
    return lax.ppermute(two, axis, [(1, 2), (2, 1)])


def gather_out(four, axis):
    return lax.ppermute(four, axis, [(1, 0), (2, 3)])


def gather_rest(four, out, axis):
    me = lax.axis_index(axis)
    half = four.shape[1] // 2
    turned = jnp.concatenate([four[:, half:], four[:, :half]], axis=1)
    return jnp.where((me == 1) | (me == 2), turned, out)


def gather_any(block, axis):
    every = lax.all_gather(block, axis, axis=0)
    n, me = lax.axis_size(axis), lax.axis_index(axis)
    return jnp.concatenate([lax.dynamic_index_in_dim(every, me ^ r, 0, keepdims=False) for r in range(n)], axis=1)


def score_kernel(scale, refs, even, odd, half_norms, offsets, out, block):
    rows = even.shape[0]

    @pl.when(pl.program_id(0) == 0)
    def _():
        block[:rows] = even[...]
        block[rows:] = odd[...]

    scores = lax.dot_general(refs[...], block[...], (((1,), (1,)), ((), ())), preferred_element_type=F32) * scale
    out[...] = jnp.exp(scores - half_norms[...] - offsets[...]).astype(BF16)


def score_block(refs, even, odd, half_norms, offsets, scale):
    rows, width = refs.shape
    count = even.shape[0]
    tile = SCORE_ROWS if rows % SCORE_ROWS == 0 else rows
    return pl.pallas_call(
        functools.partial(score_kernel, scale),
        out_shape=jax.ShapeDtypeStruct((rows, 2 * count), BF16),
        grid=(rows // tile,),
        in_specs=[
            pl.BlockSpec((tile, width), lambda i: (i, 0)),
            pl.BlockSpec((count, width), lambda i: (0, 0)),
            pl.BlockSpec((count, width), lambda i: (0, 0)),
            pl.BlockSpec((tile, 1), lambda i: (i, 0)),
            pl.BlockSpec((1, 2 * count), lambda i: (0, 0)),
        ],
        out_specs=pl.BlockSpec((tile, 2 * count), lambda i: (i, 0)),
        scratch_shapes=[pltpu.VMEM((2 * count, width), BF16)],
        compiler_params=pltpu.CompilerParams(vmem_limit_bytes=24 * 1024 * 1024),
        cost_estimate=pl.CostEstimate(flops=SCORE_COST, bytes_accessed=SCORE_COST, transcendentals=0),
        name="scores",
    )(refs, even, odd, half_norms, offsets)


def body(images, exponents, references, partners):
    rows, width = references.shape
    half = rows // 2
    count = lax.axis_size("ref")
    me = lax.axis_index("ref")
    planes = lax.axis_size("img")
    plane = lax.axis_index("img")
    img_rows = images.shape[0]
    total_images = img_rows * count * planes
    top = count // 2
    upper = me // top
    apart = top // 2
    columns = width // planes

    pieces = {0: images}
    for k in reversed(range(2, count, 2)):
        if k & (k - 1) == 0:
            pieces[k] = swap(images, "ref", k)
    pieces[1] = swap(images, "ref", 1)

    def of_plane(array, z):
        return lax.dynamic_slice_in_dim(array, z * columns, columns, axis=1)

    line = planes == 4
    far = {}
    if line:
        near = swap(jnp.concatenate([of_plane(images, plane ^ 1), of_plane(images, plane ^ 3)], axis=1), "img", 1)
        pieces[1] = after(pieces[1], near)
        onward = jnp.concatenate([of_plane(images, plane ^ 2), near[:, columns:]], axis=0)
        onward = swap(onward, "img", 2)
    else:
        far[0] = jnp.concatenate([swap(of_plane(images, plane ^ r), "img", r) for r in range(1, planes)], axis=0)

    kept = half * HALVED // 6
    both = half - kept
    own_order = jnp.arange(rows, dtype=jnp.int32)
    pair = partners % rows
    mirrored = jnp.where(
        pair < half,
        jnp.where(pair < kept, pair + half + both, pair + both),
        jnp.where(pair < half + both, pair - both, pair - half - both),
    )
    place = jnp.where(upper == 0, own_order, mirrored)
    one_hot = (own_order[:, None] == place[None, :]).astype(BF16)
    refs = jnp.dot(one_hot, references, preferred_element_type=F32).astype(BF16)
    half_norms = 0.5 * (jnp.sum(jnp.square(refs.astype(F32)), axis=1, keepdims=True) / width)
    offsets = exponents.reshape(count, img_rows)[me ^ jnp.arange(count)].astype(F32) * 0.25
    offsets = offsets.reshape(count // 2, 1, 2 * img_rows)
    scale = 1.0 / jnp.sqrt(F32(total_images))

    weights, sent = {}, {}

    def score(m):
        even, odd = pieces[2 * m], pieces[2 * m + 1]
        weights[m] = score_block(refs, even, odd, half_norms, offsets[m], 1.0 / math.sqrt(width))

    def send(m):
        start = half + both if m < apart else kept
        sent[m ^ apart] = swap(weights[m][start:], "ref", top)

    def mean(a, b):
        return (0.5 * a.astype(F32) + 0.5 * b.astype(F32)).astype(BF16)

    def kept_sums(ms, at):
        w = [mean(weights[m][:kept], sent[m][-kept:])[at] for m in ms]
        x = [pieces[k] for m in ms for k in (2 * m, 2 * m + 1)]
        return jnp.dot(jnp.concatenate(w, axis=1), jnp.concatenate(x, axis=0), preferred_element_type=F32)

    def both_weights(m):
        theirs = jnp.concatenate([sent[m][both : 2 * both], sent[m][:both]], axis=0)
        return mean(weights[m][kept : half + both], theirs)

    def both_sums(m, w):
        xs = [of_plane(pieces[2 * m], plane), of_plane(pieces[2 * m + 1], plane)]
        for r in range(planes - 1):
            xs += [far[k][r * img_rows : (r + 1) * img_rows] for k in (2 * m, 2 * m + 1)]
        return jnp.dot(w, jnp.concatenate(xs, axis=0), preferred_element_type=F32)

    blocks = count // 2
    last = [m for m in range(blocks) if m | apart == blocks - 1]
    first = [m for m in range(blocks) if m not in last]
    early_both = [m for m in first if m < apart]
    late_both = [m for m in last if m < apart]
    end = blocks - 1

    score(0)
    send(0)
    singles = [m for m in reversed(range(1, blocks)) if m & (m - 1) == 0]
    before = weights[0]
    for m in singles:
        pieces[2 * m] = after(pieces[2 * m], before)
        pieces[2 * m + 1] = swap(pieces[2 * m], "ref", 1)
        before = pieces[2 * m]
    for m in range(1, blocks):
        if m & (m - 1):
            k = 2 * m
            pieces[k] = swap(pieces[k ^ (k & -k)], "ref", k & -k)
            if m != end:
                pieces[k + 1] = swap(pieces[k], "ref", 1)
    for m in sorted(range(1, end), reverse=True):
        if m == 1:
            pieces[2] = after(pieces[2], weights[apart], sent[apart])
        score(m)
        send(m)
    ends = {m: gather_ends(both_weights(m), "img") for m in early_both} if line else {}
    early = kept_sums(first, slice(None))
    pieces[2 * end] = after(pieces[2 * end], early, *ends.values())
    pieces[2 * end + 1] = swap(pieces[2 * end], "ref", 1)
    score(end)
    send(end)
    if line:
        far[0] = jnp.concatenate([near[:, :columns], after(onward, weights[end])], axis=0)
    free = after(far[0], pieces[2 * end])
    for f in range(2, top, 2):
        far[f] = swap(far[f ^ (f & -f)] if f & (f - 1) else free, "ref", f & -f)
    middles = {m: gather_middle(ends[m], "img") for m in ends}
    at = end ^ apart
    middles = {m: after(middles[m], sent[at]) for m in middles}
    outs = {m: gather_out(middles[m], "img") for m in middles}
    late = {m: both_weights(m) for m in late_both}
    late_ends = {m: gather_ends(late[m], "img") for m in late_both} if line else {}

    parts = []
    chunk = kept // ROW_CHUNKS
    for c in range(ROW_CHUNKS):
        at = slice(c * chunk, (c + 1) * chunk)
        parts.append((early[at] + kept_sums(last, at)) * scale)
    pairs = [halves(part, "img", 1) for part in parts]
    if line:
        late_ends = {m: after(late_ends[m], *parts) for m in late_both}
        late_middles = {m: gather_middle(late_ends[m], "img") for m in late_both}
    came = [swap(give, "img", 1) for keep, give in pairs]
    for f in range(0, top, 2):
        far[f] = after(far[f], *[give for keep, give in pairs])
        far[f + 1] = swap(far[f], "ref", 1)
    parts = [pairs[0][0] + came[0].astype(F32)]
    if line:
        late_middles = {m: after(late_middles[m], parts[0]) for m in late_both}
        late_outs = {m: gather_out(late_middles[m], "img") for m in late_both}
        came[1:] = [after(block, *late_middles.values()) for block in came[1:]]
    parts += [keep + block.astype(F32) for (keep, give), block in zip(pairs[1:], came[1:])]
    bit = 2
    while bit < planes:
        pairs = [halves(part, "img", bit) for part in parts]
        parts = [keep + swap(give, "img", bit).astype(F32) for keep, give in pairs]
        bit *= 2
    if line:
        late_outs = {m: after(late_outs[m], parts[0]) for m in late_both}
    if line:
        ends.update(late_ends)
        middles.update(late_middles)
        outs.update(late_outs)
        gathered = {m: jnp.concatenate([ends[m], gather_rest(middles[m], outs[m], "img")], axis=1) for m in ends}
    else:
        gathered = {m: gather_any(both_weights(m), "img") for m in range(apart)}
    shared = sum(both_sums(m, gathered[m]) for m in range(apart)) * scale
    theirs = swap(shared.astype(BF16), "ref", top).astype(F32)
    shared = shared + jnp.concatenate([theirs[both:], theirs[:both]], axis=0)
    other = [swap(part.astype(BF16), "ref", top).astype(F32) for part in parts]
    return jnp.concatenate(parts + [shared] + other, axis=0).at[place].get(mode="promise_in_bounds")


def solution(mesh):
    in_specs = (P(("img", "ref"), None), P("img"), P("ref", None), P("ref"))
    out_specs = P("ref", "img")
    return jax.shard_map(body, mesh=mesh, in_specs=in_specs, out_specs=out_specs, check_vma=False)
```

```python
import jax
import jax.numpy as jnp
from jax import lax
from jax.sharding import PartitionSpec as P

F32 = jnp.float32
BF16 = jnp.bfloat16
ROW_CHUNKS = (7, 7, 6, 4)
FORWARD_LOW = 3


def swap(block, axis, bit):
    count = lax.axis_size(axis)
    return lax.ppermute(block, axis, [(i, i ^ bit) for i in range(count)])


def after(array, *others):
    return lax.optimization_barrier((array, *others))[0]


def halves(part, axis, bit):
    n = lax.axis_size(axis)
    side = lax.axis_index(axis) // bit % 2
    blocks = n // bit
    width = part.shape[1] // blocks

    def of_side(s):
        cut = [lax.dynamic_slice_in_dim(part, (2 * j + s) * width, width, axis=1) for j in range(blocks // 2)]
        return jnp.concatenate(cut, axis=1)

    return of_side(side), of_side(1 - side).astype(BF16)


def body(images, exponents, references, partners):
    rows, width = references.shape
    half = rows // 2
    count = lax.axis_size("ref")
    me = lax.axis_index("ref")
    img_rows = images.shape[0]
    total_images = img_rows * count * lax.axis_size("img")
    top = count // 2
    upper = me // top

    pieces = {0: [images]}
    for k in reversed(range(2, count, 2)):
        if k & (k - 1) == 0:
            pieces[k] = [swap(images, "ref", k)]
    pieces[1] = [swap(images, "ref", 1)]

    own_order = jnp.arange(rows, dtype=jnp.int32)
    place = jnp.where(upper == 0, own_order, partners % rows)
    place = (place + upper * half) % rows
    one_hot = (own_order[:, None] == place[None, :]).astype(BF16)
    refs = jnp.dot(one_hot, references, preferred_element_type=F32).astype(BF16)
    norms = jnp.sum(jnp.square(refs.astype(F32)), axis=1) / width
    inv_root = 1.0 / jnp.sqrt(F32(width))
    offsets = exponents.reshape(count, img_rows)[me ^ jnp.arange(count)].astype(F32) * 0.25

    apart = top // 2
    blocks = count // 2
    end = blocks - 1
    weights, sent = {}, {}

    def images_of(ms):
        return jnp.concatenate([part for m in ms for k in (2 * m, 2 * m + 1) for part in pieces[k]], axis=0)

    def score(m):
        scores = lax.dot_general(refs, images_of([m]), (((1,), (1,)), ((), ())), preferred_element_type=F32) * inv_root
        scores = scores - 0.5 * norms[:, None] - offsets[2 * m : 2 * m + 2].reshape(1, 2 * img_rows)
        weights[m] = jnp.exp(scores).astype(BF16)

    def send(m):
        sent[m ^ apart] = swap(weights[m][half:], "ref", top)

    def mean(m):
        return (0.5 * weights[m][:half].astype(F32) + 0.5 * sent[m].astype(F32)).astype(BF16)

    score(0)
    singles = [k for k in reversed(range(2, count, 2)) if k & (k - 1) == 0]
    for k in singles:
        pieces[k] = [after(pieces[k][0], weights[0])]
    cut = img_rows * FORWARD_LOW // 4
    for k in range(2, count, 2):
        if k not in singles:
            low, high = k & -k, 1 << (k.bit_length() - 1)
            whole = [jnp.concatenate(pieces[k ^ bit], axis=0) for bit in (low, high)]
            pieces[k] = [swap(whole[0][:cut], "ref", low), swap(whole[1][cut:], "ref", high)]
        if k != 2 * end:
            pieces[k + 1] = [swap(part, "ref", 1) for part in pieces[k]]
    own = weights[0]
    weights[0] = after(own, *pieces[top + 1])
    send(0)
    weights[0] = own
    for m in reversed(range(1, end)):
        score(m)
        send(m)
    pieces[2 * end] = [after(part, *weights.values()) for part in pieces[2 * end]]
    pieces[2 * end + 1] = [swap(part, "ref", 1) for part in pieces[2 * end]]
    score(end)
    send(end)

    last = [m for m in range(blocks) if m | apart == end]
    first = [m for m in range(blocks) if m not in last]
    w = after(jnp.concatenate([mean(m) for m in first], axis=1), weights[end])
    early = jnp.dot(w, images_of(first), preferred_element_type=F32)
    w = jnp.concatenate([mean(m) for m in last], axis=1)
    late_images = images_of(last)

    scale = 1.0 / jnp.sqrt(F32(total_images))
    unit = half // sum(ROW_CHUNKS)
    pairs = []
    start = 0
    for size in ROW_CHUNKS:
        at = slice(start, start + size * unit)
        start += size * unit
        rows_w = after(w[at], pairs[-1][1]) if pairs else w[at]
        late = jnp.dot(rows_w, late_images, preferred_element_type=F32)
        pairs.append(halves((early[at] + late) * scale, "img", 1))
    bit = 1
    while True:
        came = [swap(give, "img", bit) for keep, give in pairs]
        bit *= 2
        going = []
        for (keep, give), block in zip(pairs, came):
            total = keep + (after(block, going[-1][1]) if going else block).astype(F32)
            going.append(halves(total, "img", bit) if bit < lax.axis_size("img") else (total, total.astype(BF16)))
        pairs = going
        if bit >= lax.axis_size("img"):
            break
    done = [keep for keep, give in pairs]
    gone = [give for keep, give in pairs]
    other = [swap(block, "ref", top).astype(F32) for block in gone]
    return jnp.concatenate(done + other, axis=0).at[place].get(mode="promise_in_bounds")


def solution(mesh):
    in_specs = (P(("img", "ref"), None), P("img"), P("ref", None), P("ref"))
    out_specs = P("ref", "img")
    return jax.shard_map(body, mesh=mesh, in_specs=in_specs, out_specs=out_specs, check_vma=False)
```

```python
import jax
import jax.numpy as jnp
from jax import lax
from jax.sharding import PartitionSpec as P

F32 = jnp.float32
BF16 = jnp.bfloat16
ROW_CHUNKS = (10, 7, 4, 3)
FORWARD_LOW = 5


def swap(block, axis, bit):
    count = lax.axis_size(axis)
    return lax.ppermute(block, axis, [(i, i ^ bit) for i in range(count)])


def after(array, *others):
    return lax.optimization_barrier((array, *others))[0]


def halves(part, axis, bit):
    n = lax.axis_size(axis)
    side = lax.axis_index(axis) // bit % 2
    blocks = n // bit
    width = part.shape[1] // blocks

    def of_side(s):
        cut = [lax.dynamic_slice_in_dim(part, (2 * j + s) * width, width, axis=1) for j in range(blocks // 2)]
        return jnp.concatenate(cut, axis=1)

    return of_side(side), of_side(1 - side).astype(BF16)


def body(images, exponents, references, partners):
    rows, width = references.shape
    half = rows // 2
    count = lax.axis_size("ref")
    me = lax.axis_index("ref")
    img_rows = images.shape[0]
    total_images = img_rows * count * lax.axis_size("img")
    top = count // 2
    upper = me // top

    pieces = {0: [images]}
    for k in reversed(range(2, count, 2)):
        if k & (k - 1) == 0:
            pieces[k] = [swap(images, "ref", k)]
    pieces[1] = [swap(images, "ref", 1)]

    own_order = jnp.arange(rows, dtype=jnp.int32)
    place = jnp.where(upper == 0, own_order, partners % rows)
    place = (place + upper * half) % rows
    one_hot = (own_order[:, None] == place[None, :]).astype(BF16)
    refs = jnp.dot(one_hot, references, preferred_element_type=F32).astype(BF16)
    norms = jnp.sum(jnp.square(refs.astype(F32)), axis=1) / width
    inv_root = 1.0 / jnp.sqrt(F32(width))
    offsets = exponents.reshape(count, img_rows)[me ^ jnp.arange(count)].astype(F32) * 0.25

    apart = top // 2
    blocks = count // 2
    end = blocks - 1
    weights, sent = {}, {}

    def images_of(ms):
        return jnp.concatenate([part for m in ms for k in (2 * m, 2 * m + 1) for part in pieces[k]], axis=0)

    def score(m):
        scores = lax.dot_general(refs, images_of([m]), (((1,), (1,)), ((), ())), preferred_element_type=F32) * inv_root
        scores = scores - 0.5 * norms[:, None] - offsets[2 * m : 2 * m + 2].reshape(1, 2 * img_rows)
        weights[m] = jnp.exp(scores).astype(BF16)

    unit = half // sum(ROW_CHUNKS)
    ends = [0]
    for size in ROW_CHUNKS:
        ends.append(ends[-1] + size * unit)
    chunks = [slice(*pair) for pair in zip(ends, ends[1:])]

    def send(m, cuts):
        sent[m ^ apart] = [swap(weights[m][half + start : half + stop], "ref", top) for start, stop in cuts]

    def mean(m, at):
        return (0.5 * weights[m][at].astype(F32) + 0.5 * jnp.concatenate(sent[m], axis=0)[at].astype(F32)).astype(BF16)

    score(0)
    singles = [k for k in reversed(range(2, count, 2)) if k & (k - 1) == 0]
    for k in singles:
        pieces[k] = [after(pieces[k][0], weights[0])]
    cut = img_rows * FORWARD_LOW // 8
    for k in range(2, count, 2):
        if k not in singles:
            low, high = k & -k, 1 << (k.bit_length() - 1)
            whole = [jnp.concatenate(pieces[k ^ bit], axis=0) for bit in (low, high)]
            pieces[k] = [swap(whole[0][:cut], "ref", low), swap(whole[1][cut:], "ref", high)]
        if k != 2 * end:
            pieces[k + 1] = [swap(part, "ref", 1) for part in pieces[k]]
    whole = [(0, half)]
    send(0, whole)
    for m in reversed(range(1, end)):
        score(m)
        send(m, whole)
    pieces[2 * end] = [after(part, *weights.values()) for part in pieces[2 * end]]
    pieces[2 * end + 1] = [swap(part, "ref", 1) for part in pieces[2 * end]]
    pieces[2 * end][0] = after(pieces[2 * end][0], sent[end][0])
    score(end)
    send(end, [(0, ends[1]), (ends[1], half)])

    order = range(blocks)
    every_image = images_of(order)
    scale = 1.0 / jnp.sqrt(F32(total_images))
    pairs = []
    for at in chunks:
        w = jnp.concatenate([mean(m, at) for m in order], axis=1)
        if pairs:
            w = after(w, pairs[-1][1])
        pairs.append(halves(jnp.dot(w, every_image, preferred_element_type=F32) * scale, "img", 1))
    bit = 1
    while True:
        came = [swap(give, "img", bit) for keep, give in pairs]
        bit *= 2
        going = []
        for (keep, give), block in zip(pairs, came):
            total = keep + (after(block, going[-1][1]) if going else block).astype(F32)
            going.append(halves(total, "img", bit) if bit < lax.axis_size("img") else (total, total.astype(BF16)))
        pairs = going
        if bit >= lax.axis_size("img"):
            break
    done = [keep for keep, give in pairs]
    gone = [give for keep, give in pairs]
    other = [swap(block, "ref", top).astype(F32) for block in gone]
    return jnp.concatenate(done + other, axis=0).at[place].get(mode="promise_in_bounds")


def solution(mesh):
    in_specs = (P(("img", "ref"), None), P("img"), P("ref", None), P("ref"))
    out_specs = P("ref", "img")
    return jax.shard_map(body, mesh=mesh, in_specs=in_specs, out_specs=out_specs, check_vma=False)
```

```python
import jax
import jax.numpy as jnp
from jax import lax
from jax.sharding import PartitionSpec as P

F32 = jnp.float32
BF16 = jnp.bfloat16
ROW_CHUNKS = (5, 6, 6, 4, 3)
FORWARD_LOW = 5


def swap(block, axis, bit):
    count = lax.axis_size(axis)
    return lax.ppermute(block, axis, [(i, i ^ bit) for i in range(count)])


def after(array, *others):
    return lax.optimization_barrier((array, *others))[0]


def halves(part, axis, bit):
    n = lax.axis_size(axis)
    side = lax.axis_index(axis) // bit % 2
    blocks = n // bit
    width = part.shape[1] // blocks

    def of_side(s):
        cut = [lax.dynamic_slice_in_dim(part, (2 * j + s) * width, width, axis=1) for j in range(blocks // 2)]
        return jnp.concatenate(cut, axis=1)

    return of_side(side), of_side(1 - side).astype(BF16)


def body(images, exponents, references, partners):
    rows, width = references.shape
    half = rows // 2
    count = lax.axis_size("ref")
    me = lax.axis_index("ref")
    img_rows = images.shape[0]
    total_images = img_rows * count * lax.axis_size("img")
    top = count // 2
    upper = me // top

    pieces = {0: [images]}
    for k in reversed(range(2, count, 2)):
        if k & (k - 1) == 0:
            pieces[k] = [swap(images, "ref", k)]
    pieces[1] = [swap(images, "ref", 1)]

    own_order = jnp.arange(rows, dtype=jnp.int32)
    place = jnp.where(upper == 0, own_order, partners % rows)
    place = (place + upper * half) % rows
    one_hot = (own_order[:, None] == place[None, :]).astype(BF16)
    refs = jnp.dot(one_hot, references, preferred_element_type=F32).astype(BF16)
    norms = jnp.sum(jnp.square(refs.astype(F32)), axis=1) / width
    inv_root = 1.0 / jnp.sqrt(F32(width))
    offsets = exponents.reshape(count, img_rows)[me ^ jnp.arange(count)].astype(F32) * 0.25

    apart = top // 2
    blocks = count // 2
    end = blocks - 1
    weights, sent = {}, {}

    def images_of(ms):
        return jnp.concatenate([part for m in ms for k in (2 * m, 2 * m + 1) for part in pieces[k]], axis=0)

    def score(m):
        scores = lax.dot_general(refs, images_of([m]), (((1,), (1,)), ((), ())), preferred_element_type=F32) * inv_root
        scores = scores - 0.5 * norms[:, None] - offsets[2 * m : 2 * m + 2].reshape(1, 2 * img_rows)
        weights[m] = jnp.exp(scores).astype(BF16)

    unit = half // sum(ROW_CHUNKS)
    ends = [0]
    for size in ROW_CHUNKS:
        ends.append(ends[-1] + size * unit)
    chunks = [slice(*pair) for pair in zip(ends, ends[1:])]

    def send(m, cuts):
        parts = [weights[m][half + start : half + stop] for start, stop in cuts]
        parts[1:] = [after(part, *sent[m]) for part in parts[1:]]
        sent[m ^ apart] = [swap(part, "ref", top) for part in parts]

    def mean(m, at):
        return (0.5 * weights[m][at].astype(F32) + 0.5 * jnp.concatenate(sent[m], axis=0)[at].astype(F32)).astype(BF16)

    score(0)
    singles = [k for k in reversed(range(2, count, 2)) if k & (k - 1) == 0]
    for k in singles:
        pieces[k] = [after(pieces[k][0], weights[0], *(pieces[2 * k + 1] if k != singles[0] else []))]
        pieces[k + 1] = [swap(pieces[k][0], "ref", 1)]
    cut = img_rows * FORWARD_LOW // 8
    for k in range(2, count, 2):
        if k not in singles:
            low, high = k & -k, 1 << (k.bit_length() - 1)
            whole = [jnp.concatenate(pieces[k ^ bit], axis=0) for bit in (low, high)]
            pieces[k] = [swap(whole[0][:cut], "ref", low), swap(whole[1][cut:], "ref", high)]
        if k + 1 not in pieces and k != 2 * end:
            pieces[k + 1] = [swap(part, "ref", 1) for part in pieces[k]]
    whole = [(0, half)]
    send(0, whole)
    for m in reversed(range(1, end)):
        score(m)
        send(m, whole)
    pieces[2 * end] = [after(part, *weights.values()) for part in pieces[2 * end]]
    pieces[2 * end + 1] = [swap(part, "ref", 1) for part in pieces[2 * end]]
    score(end)
    send(end, [(0, ends[1]), (ends[1], half)])

    order = range(blocks)
    every_image = images_of(order)
    scale = 1.0 / jnp.sqrt(F32(total_images))
    def onward(pair, block, bit, before):
        total = pair[0] + after(block, *before).astype(F32)
        return halves(total, "img", bit) if bit < lax.axis_size("img") else (total, total.astype(BF16))

    first, came, pairs = [], [], []
    for c, at in enumerate(chunks):
        w = jnp.concatenate([mean(m, at) for m in order], axis=1)
        w = after(w, *[give for keep, give in first[-1:] + (pairs[-1:] if c > 1 else [])])
        first.append(halves(jnp.dot(w, every_image, preferred_element_type=F32) * scale, "img", 1))
        came.append(swap(first[c][1], "img", 1))
        if c:
            pairs.append(onward(first[c - 1], came[c - 1], 2, [give for keep, give in pairs[-1:]]))
    pairs.append(onward(first[-1], came[-1], 2, [pairs[-1][1]]))
    bit = 2
    while bit < lax.axis_size("img"):
        came = [swap(give, "img", bit) for keep, give in pairs]
        bit *= 2
        after_it = []
        for pair, block in zip(pairs, came):
            after_it.append(onward(pair, block, bit, [give for keep, give in after_it[-1:]]))
        pairs = after_it
    done = [keep for keep, give in pairs]
    gone = [give for keep, give in pairs]
    other = [swap(block, "ref", top).astype(F32) for block in gone]
    return jnp.concatenate(done + other, axis=0).at[place].get(mode="promise_in_bounds")


def solution(mesh):
    in_specs = (P(("img", "ref"), None), P("img"), P("ref", None), P("ref"))
    out_specs = P("ref", "img")
    return jax.shard_map(body, mesh=mesh, in_specs=in_specs, out_specs=out_specs, check_vma=False)
```

```python
import jax
import jax.numpy as jnp
from jax import lax
from jax.sharding import PartitionSpec as P

F32 = jnp.float32
BF16 = jnp.bfloat16
ROW_CHUNKS = (5, 6, 6, 4, 3)
FORWARD_LOW = 5


def swap(block, axis, bit):
    count = lax.axis_size(axis)
    return lax.ppermute(block, axis, [(i, i ^ bit) for i in range(count)])


def after(array, *others):
    return lax.optimization_barrier((array, *others))[0]


def halves(part, axis, bit):
    n = lax.axis_size(axis)
    side = lax.axis_index(axis) // bit % 2
    blocks = n // bit
    width = part.shape[1] // blocks

    def of_side(s):
        cut = [lax.dynamic_slice_in_dim(part, (2 * j + s) * width, width, axis=1) for j in range(blocks // 2)]
        return jnp.concatenate(cut, axis=1)

    return of_side(side), of_side(1 - side).astype(BF16)


def body(images, exponents, references, partners):
    rows, width = references.shape
    half = rows // 2
    count = lax.axis_size("ref")
    me = lax.axis_index("ref")
    img_rows = images.shape[0]
    total_images = img_rows * count * lax.axis_size("img")
    top = count // 2
    upper = me // top

    pieces = {0: [images]}
    for k in reversed(range(2, count, 2)):
        if k & (k - 1) == 0:
            pieces[k] = [swap(images, "ref", k)]
    pieces[1] = [swap(images, "ref", 1)]

    own_order = jnp.arange(rows, dtype=jnp.int32)
    place = jnp.where(upper == 0, own_order, partners % rows)
    place = (place + upper * half) % rows
    one_hot = (own_order[:, None] == place[None, :]).astype(BF16)
    refs = jnp.dot(one_hot, references, preferred_element_type=F32).astype(BF16)
    norms = jnp.sum(jnp.square(refs.astype(F32)), axis=1) / width
    inv_root = 1.0 / jnp.sqrt(F32(width))
    offsets = exponents.reshape(count, img_rows)[me ^ jnp.arange(count)].astype(F32) * 0.25

    apart = top // 2
    blocks = count // 2
    end = blocks - 1
    weights, sent = {}, {}

    def images_of(ms):
        return jnp.concatenate([part for m in ms for k in (2 * m, 2 * m + 1) for part in pieces[k]], axis=0)

    def score(m):
        scores = lax.dot_general(refs, images_of([m]), (((1,), (1,)), ((), ())), preferred_element_type=F32) * inv_root
        scores = scores - 0.5 * norms[:, None] - offsets[2 * m : 2 * m + 2].reshape(1, 2 * img_rows)
        weights[m] = jnp.exp(scores).astype(BF16)

    unit = half // sum(ROW_CHUNKS)
    ends = [0]
    for size in ROW_CHUNKS:
        ends.append(ends[-1] + size * unit)
    chunks = [slice(*pair) for pair in zip(ends, ends[1:])]

    def send(m, cuts):
        came = []
        for start, stop in cuts:
            came.append(swap(after(weights[m][half + start : half + stop], *came), "ref", top))
        sent[m ^ apart] = came

    def mean(m, at):
        return (0.5 * weights[m][at].astype(F32) + 0.5 * jnp.concatenate(sent[m], axis=0)[at].astype(F32)).astype(BF16)

    score(0)
    singles = [k for k in reversed(range(2, count, 2)) if k & (k - 1) == 0]
    for k in singles:
        pieces[k] = [after(pieces[k][0], weights[0], *(pieces[2 * k + 1] if k != singles[0] else []))]
        pieces[k + 1] = [swap(pieces[k][0], "ref", 1)]
    cut = img_rows * FORWARD_LOW // 8
    for k in range(2, count, 2):
        if k not in singles:
            low, high = k & -k, 1 << (k.bit_length() - 1)
            whole = [jnp.concatenate(pieces[k ^ bit], axis=0) for bit in (low, high)]
            pieces[k] = [swap(whole[0][:cut], "ref", low), swap(whole[1][cut:], "ref", high)]
        if k + 1 not in pieces and k != 2 * end:
            pieces[k + 1] = [swap(part, "ref", 1) for part in pieces[k]]
    whole = [(0, half)]
    send(0, whole)
    for m in reversed(range(1, end)):
        score(m)
        send(m, whole)
    sent[apart] = [after(part, *weights.values()) for part in sent[apart]]
    pieces[2 * end] = [after(part, *weights.values()) for part in pieces[2 * end]]
    pieces[2 * end + 1] = [swap(part, "ref", 1) for part in pieces[2 * end]]
    score(end)
    for m in sent:
        if m != apart:
            sent[m] = [after(part, weights[end]) for part in sent[m]]
    send(end, [(0, ends[1]), (ends[1], half)])

    order = range(blocks)
    every_image = images_of(order)
    scale = 1.0 / jnp.sqrt(F32(total_images))
    def onward(pair, block, bit, before):
        total = pair[0] + after(block, *before).astype(F32)
        return halves(total, "img", bit) if bit < lax.axis_size("img") else (total, total.astype(BF16))

    first, came, pairs = [], [], []
    for c, at in enumerate(chunks):
        w = jnp.concatenate([mean(m, at) for m in order], axis=1)
        w = after(w, *[give for keep, give in first[-1:] + (pairs[-1:] if c > 1 else [])])
        first.append(halves(jnp.dot(w, every_image, preferred_element_type=F32) * scale, "img", 1))
        came.append(swap(first[c][1], "img", 1))
        if c:
            pairs.append(onward(first[c - 1], came[c - 1], 2, [give for keep, give in pairs[-1:]]))
    pairs.append(onward(first[-1], came[-1], 2, [pairs[-1][1]]))
    bit = 2
    while bit < lax.axis_size("img"):
        came = [swap(give, "img", bit) for keep, give in pairs]
        bit *= 2
        after_it = []
        for pair, block in zip(pairs, came):
            after_it.append(onward(pair, block, bit, [give for keep, give in after_it[-1:]]))
        pairs = after_it
    done = [keep for keep, give in pairs]
    gone = [give for keep, give in pairs]
    other = [swap(block, "ref", top).astype(F32) for block in gone]
    return jnp.concatenate(done + other, axis=0).at[place].get(mode="promise_in_bounds")


def solution(mesh):
    in_specs = (P(("img", "ref"), None), P("img"), P("ref", None), P("ref"))
    out_specs = P("ref", "img")
    return jax.shard_map(body, mesh=mesh, in_specs=in_specs, out_specs=out_specs, check_vma=False)
```

```python
import jax
import jax.numpy as jnp
from jax import lax
from jax.sharding import PartitionSpec as P

F32 = jnp.float32
BF16 = jnp.bfloat16
ROW_CHUNKS = (7, 6, 5, 3, 3)
FORWARD_LOW = 4


def swap(block, axis, bit):
    count = lax.axis_size(axis)
    return lax.ppermute(block, axis, [(i, i ^ bit) for i in range(count)])


def after(array, *others):
    return lax.optimization_barrier((array, *others))[0]


def halves(part, axis, bit):
    n = lax.axis_size(axis)
    side = lax.axis_index(axis) // bit % 2
    blocks = n // bit
    width = part.shape[1] // blocks

    def of_side(s):
        cut = [lax.dynamic_slice_in_dim(part, (2 * j + s) * width, width, axis=1) for j in range(blocks // 2)]
        return jnp.concatenate(cut, axis=1)

    return of_side(side), of_side(1 - side).astype(BF16)


def body(images, exponents, references, partners):
    rows, width = references.shape
    half = rows // 2
    count = lax.axis_size("ref")
    me = lax.axis_index("ref")
    img_rows = images.shape[0]
    total_images = img_rows * count * lax.axis_size("img")
    top = count // 2
    upper = me // top

    pieces = {0: [images]}
    for k in reversed(range(2, count, 2)):
        if k & (k - 1) == 0:
            pieces[k] = [swap(images, "ref", k)]
    pieces[1] = [swap(images, "ref", 1)]

    own_order = jnp.arange(rows, dtype=jnp.int32)
    place = jnp.where(upper == 0, own_order, partners % rows)
    place = (place + upper * half) % rows
    one_hot = (own_order[:, None] == place[None, :]).astype(BF16)
    refs = jnp.dot(one_hot, references, preferred_element_type=F32).astype(BF16)
    norms = jnp.sum(jnp.square(refs.astype(F32)), axis=1) / width
    inv_root = 1.0 / jnp.sqrt(F32(width))
    offsets = exponents.reshape(count, img_rows)[me ^ jnp.arange(count)].astype(F32) * 0.25

    apart = top // 2
    blocks = count // 2
    end = blocks - 1
    weights, sent = {}, {}

    def images_of(ms):
        return jnp.concatenate([part for m in ms for k in (2 * m, 2 * m + 1) for part in pieces[k]], axis=0)

    def score(m):
        scores = lax.dot_general(refs, images_of([m]), (((1,), (1,)), ((), ())), preferred_element_type=F32) * inv_root
        scores = scores - 0.5 * norms[:, None] - offsets[2 * m : 2 * m + 2].reshape(1, 2 * img_rows)
        weights[m] = jnp.exp(scores).astype(BF16)

    unit = half // sum(ROW_CHUNKS)
    ends = [0]
    for size in ROW_CHUNKS:
        ends.append(ends[-1] + size * unit)
    chunks = [slice(*pair) for pair in zip(ends, ends[1:])]

    early = ends[1]

    def send(m):
        sent[m ^ apart] = swap(weights[m][half : half + early], "ref", top)

    def mean(m, at):
        if at.stop <= early:
            theirs = sent[m][at]
        else:
            theirs = rest[at.start - early : at.stop - early, 2 * img_rows * m : 2 * img_rows * (m + 1)]
        return (0.5 * weights[m][at].astype(F32) + 0.5 * theirs.astype(F32)).astype(BF16)

    score(0)
    singles = [k for k in reversed(range(2, count, 2)) if k & (k - 1) == 0]
    for k in singles:
        pieces[k] = [after(pieces[k][0], weights[0], *(pieces[2 * k + 1] if k != singles[0] else []))]
        pieces[k + 1] = [swap(pieces[k][0], "ref", 1)]
    cut = img_rows * FORWARD_LOW // 8
    for k in range(2, count, 2):
        if k not in singles:
            low, high = k & -k, 1 << (k.bit_length() - 1)
            whole = [jnp.concatenate(pieces[k ^ bit], axis=0) for bit in (low, high)]
            pieces[k] = [swap(whole[0][:cut], "ref", low), swap(whole[1][cut:], "ref", high)]
        if k + 1 not in pieces and k != 2 * end:
            pieces[k + 1] = [swap(part, "ref", 1) for part in pieces[k]]
    send(0)
    for m in reversed(range(1, end)):
        score(m)
        send(m)
    sent[apart] = after(sent[apart], *weights.values())
    pieces[2 * end] = [after(part, *weights.values()) for part in pieces[2 * end]]
    pieces[2 * end + 1] = [swap(part, "ref", 1) for part in pieces[2 * end]]
    score(end)
    for m in sent:
        if m != apart:
            sent[m] = after(sent[m], weights[end])
    send(end)
    rest = jnp.concatenate([weights[m ^ apart][half + early :] for m in range(blocks)], axis=1)
    rest = swap(after(rest, sent[end ^ apart]), "ref", top)

    order = range(blocks)
    every_image = images_of(order)
    scale = 1.0 / jnp.sqrt(F32(total_images))
    def onward(pair, block, bit, before):
        total = pair[0] + after(block, *before).astype(F32)
        return halves(total, "img", bit) if bit < lax.axis_size("img") else (total, total.astype(BF16))

    first, came, pairs = [], [], []
    for c, at in enumerate(chunks):
        w = jnp.concatenate([mean(m, at) for m in order], axis=1)
        w = after(w, *[give for keep, give in first[-1:] + (pairs[-1:] if c > 1 else [])])
        first.append(halves(jnp.dot(w, every_image, preferred_element_type=F32) * scale, "img", 1))
        came.append(swap(first[c][1], "img", 1))
        if c:
            pairs.append(onward(first[c - 1], came[c - 1], 2, [give for keep, give in pairs[-1:]]))
    pairs.append(onward(first[-1], came[-1], 2, [pairs[-1][1]]))
    bit = 2
    while bit < lax.axis_size("img"):
        came = [swap(give, "img", bit) for keep, give in pairs]
        bit *= 2
        after_it = []
        for pair, block in zip(pairs, came):
            after_it.append(onward(pair, block, bit, [give for keep, give in after_it[-1:]]))
        pairs = after_it
    done = [keep for keep, give in pairs]
    gone = [give for keep, give in pairs]
    other = [swap(block, "ref", top).astype(F32) for block in gone]
    return jnp.concatenate(done + other, axis=0).at[place].get(mode="promise_in_bounds")


def solution(mesh):
    in_specs = (P(("img", "ref"), None), P("img"), P("ref", None), P("ref"))
    out_specs = P("ref", "img")
    return jax.shard_map(body, mesh=mesh, in_specs=in_specs, out_specs=out_specs, check_vma=False)
```

```python
import jax
import jax.numpy as jnp
from jax import lax
from jax.sharding import PartitionSpec as P

F32 = jnp.float32
BF16 = jnp.bfloat16
ROW_CHUNKS = (8, 6, 4, 3, 3)
FORWARD_LOW = 5


def swap(block, axis, bit):
    count = lax.axis_size(axis)
    return lax.ppermute(block, axis, [(i, i ^ bit) for i in range(count)])


def after(array, *others):
    return lax.optimization_barrier((array, *others))[0]


def halves(part, axis, bit):
    n = lax.axis_size(axis)
    side = lax.axis_index(axis) // bit % 2
    blocks = n // bit
    width = part.shape[1] // blocks

    def of_side(s):
        cut = [lax.dynamic_slice_in_dim(part, (2 * j + s) * width, width, axis=1) for j in range(blocks // 2)]
        return jnp.concatenate(cut, axis=1)

    return of_side(side), of_side(1 - side).astype(BF16)


def body(images, exponents, references, partners):
    rows, width = references.shape
    half = rows // 2
    count = lax.axis_size("ref")
    me = lax.axis_index("ref")
    img_rows = images.shape[0]
    total_images = img_rows * count * lax.axis_size("img")
    top = count // 2
    upper = me // top

    pieces = {0: [images]}
    for k in reversed(range(2, count, 2)):
        if k & (k - 1) == 0:
            pieces[k] = [swap(images, "ref", k)]
    pieces[1] = [swap(images, "ref", 1)]

    own_order = jnp.arange(rows, dtype=jnp.int32)
    place = jnp.where(upper == 0, own_order, partners % rows)
    place = (place + upper * half) % rows
    one_hot = (own_order[:, None] == place[None, :]).astype(BF16)
    refs = jnp.dot(one_hot, references, preferred_element_type=F32).astype(BF16)
    norms = jnp.sum(jnp.square(refs.astype(F32)), axis=1) / width
    inv_root = 1.0 / jnp.sqrt(F32(width))
    offsets = exponents.reshape(count, img_rows)[me ^ jnp.arange(count)].astype(F32) * 0.25

    apart = top // 2
    blocks = count // 2
    end = blocks - 1
    weights, sent = {}, {}

    def images_of(ms):
        return jnp.concatenate([part for m in ms for k in (2 * m, 2 * m + 1) for part in pieces[k]], axis=0)

    def score(m):
        scores = lax.dot_general(refs, images_of([m]), (((1,), (1,)), ((), ())), preferred_element_type=F32) * inv_root
        scores = scores - 0.5 * norms[:, None] - offsets[2 * m : 2 * m + 2].reshape(1, 2 * img_rows)
        weights[m] = jnp.exp(scores).astype(BF16)

    unit = half // sum(ROW_CHUNKS)
    ends = [0]
    for size in ROW_CHUNKS:
        ends.append(ends[-1] + size * unit)
    chunks = [slice(*pair) for pair in zip(ends, ends[1:])]

    early = ends[1]
    last = [m for m in range(blocks) if m | apart == end]

    def send(m, start, stop, *before):
        part = weights[m][half + start : half + stop]
        sent.setdefault(m ^ apart, []).append(swap(after(part, *before) if before else part, "ref", top))

    def mean(m, at):
        theirs = sent[m][0][at]
        if m in last and at.start >= early:
            theirs = sent[m][1][at.start - early : at.stop - early]
        return (0.5 * weights[m][at].astype(F32) + 0.5 * theirs.astype(F32)).astype(BF16)

    score(0)
    singles = [k for k in reversed(range(2, count, 2)) if k & (k - 1) == 0]
    for k in singles:
        pieces[k] = [after(pieces[k][0], weights[0], *(pieces[2 * k + 1] if k != singles[0] else []))]
        pieces[k + 1] = [swap(pieces[k][0], "ref", 1)]
    cut = img_rows * FORWARD_LOW // 8
    for k in range(2, count, 2):
        if k not in singles:
            low, high = k & -k, 1 << (k.bit_length() - 1)
            whole = [jnp.concatenate(pieces[k ^ bit], axis=0) for bit in (low, high)]
            pieces[k] = [swap(whole[0][:cut], "ref", low), swap(whole[1][cut:], "ref", high)]
        if k + 1 not in pieces and k != 2 * end:
            pieces[k + 1] = [swap(part, "ref", 1) for part in pieces[k]]
    send(0, 0, half)
    for m in reversed(range(1, end)):
        score(m)
        send(m, 0, early if m in last else half, *pieces[2 * end][1:])
    sent[apart] = [after(part, *weights.values()) for part in sent[apart]]
    pieces[2 * end] = [after(part, *weights.values()) for part in pieces[2 * end]]
    pieces[2 * end + 1] = [swap(part, "ref", 1) for part in pieces[2 * end]]
    score(end)
    for m in sent:
        if m != apart:
            sent[m] = [after(part, weights[end]) for part in sent[m]]
    send(end, 0, early)

    order = range(blocks)
    every_image = images_of(order)
    scale = 1.0 / jnp.sqrt(F32(total_images))
    def onward(pair, block, bit, before):
        total = pair[0] + after(block, *before).astype(F32)
        return halves(total, "img", bit) if bit < lax.axis_size("img") else (total, total.astype(BF16))

    first, came, pairs = [], [], []
    for c, at in enumerate(chunks):
        w = jnp.concatenate([mean(m, at) for m in order], axis=1)
        w = after(w, *[give for keep, give in first[-1:] + (pairs[-1:] if c > 1 else [])])
        first.append(halves(jnp.dot(w, every_image, preferred_element_type=F32) * scale, "img", 1))
        came.append(swap(first[c][1], "img", 1))
        if c == 0:
            for m in last:
                send(m, early, half, first[0][1])
        if c:
            pairs.append(onward(first[c - 1], came[c - 1], 2, [give for keep, give in pairs[-1:]]))
    pairs.append(onward(first[-1], came[-1], 2, [pairs[-1][1]]))
    bit = 2
    while bit < lax.axis_size("img"):
        came = [swap(give, "img", bit) for keep, give in pairs]
        bit *= 2
        after_it = []
        for pair, block in zip(pairs, came):
            after_it.append(onward(pair, block, bit, [give for keep, give in after_it[-1:]]))
        pairs = after_it
    done = [keep for keep, give in pairs]
    gone = [give for keep, give in pairs]
    other = [swap(block, "ref", top).astype(F32) for block in gone]
    return jnp.concatenate(done + other, axis=0).at[place].get(mode="promise_in_bounds")


def solution(mesh):
    in_specs = (P(("img", "ref"), None), P("img"), P("ref", None), P("ref"))
    out_specs = P("ref", "img")
    return jax.shard_map(body, mesh=mesh, in_specs=in_specs, out_specs=out_specs, check_vma=False)
```

```python
import jax
import jax.numpy as jnp
from jax import lax
from jax.sharding import PartitionSpec as P

F32 = jnp.float32
BF16 = jnp.bfloat16
ROW_CHUNKS = (6, 6, 5, 4, 3)
FORWARD_LOW = 5


def swap(block, axis, bit):
    count = lax.axis_size(axis)
    return lax.ppermute(block, axis, [(i, i ^ bit) for i in range(count)])


def after(array, *others):
    return lax.optimization_barrier((array, *others))[0]


def halves(part, axis, bit):
    n = lax.axis_size(axis)
    side = lax.axis_index(axis) // bit % 2
    blocks = n // bit
    width = part.shape[1] // blocks

    def of_side(s):
        cut = [lax.dynamic_slice_in_dim(part, (2 * j + s) * width, width, axis=1) for j in range(blocks // 2)]
        return jnp.concatenate(cut, axis=1)

    return of_side(side), of_side(1 - side).astype(BF16)


def body(images, exponents, references, partners):
    rows, width = references.shape
    half = rows // 2
    count = lax.axis_size("ref")
    me = lax.axis_index("ref")
    img_rows = images.shape[0]
    total_images = img_rows * count * lax.axis_size("img")
    top = count // 2
    upper = me // top

    pieces = {0: [images]}
    for k in reversed(range(2, count, 2)):
        if k & (k - 1) == 0:
            pieces[k] = [swap(images, "ref", k)]
    pieces[1] = [swap(images, "ref", 1)]

    own_order = jnp.arange(rows, dtype=jnp.int32)
    place = jnp.where(upper == 0, own_order, partners % rows)
    place = (place + upper * half) % rows
    one_hot = (own_order[:, None] == place[None, :]).astype(BF16)
    refs = jnp.dot(one_hot, references, preferred_element_type=F32).astype(BF16)
    norms = jnp.sum(jnp.square(refs.astype(F32)), axis=1) / width
    inv_root = 1.0 / jnp.sqrt(F32(width))
    offsets = exponents.reshape(count, img_rows)[me ^ jnp.arange(count)].astype(F32) * 0.25

    apart = top // 2
    blocks = count // 2
    end = blocks - 1
    weights, sent = {}, {}

    def images_of(ms):
        return jnp.concatenate([part for m in ms for k in (2 * m, 2 * m + 1) for part in pieces[k]], axis=0)

    def score(m):
        scores = lax.dot_general(refs, images_of([m]), (((1,), (1,)), ((), ())), preferred_element_type=F32) * inv_root
        scores = scores - 0.5 * norms[:, None] - offsets[2 * m : 2 * m + 2].reshape(1, 2 * img_rows)
        weights[m] = jnp.exp(scores).astype(BF16)

    unit = half // sum(ROW_CHUNKS)
    ends = [0]
    for size in ROW_CHUNKS:
        ends.append(ends[-1] + size * unit)
    chunks = [slice(*pair) for pair in zip(ends, ends[1:])]

    early = ends[1]
    last = [m for m in range(blocks) if m | apart == end]

    def send(m, start, stop, *before):
        part = weights[m][half + start : half + stop]
        sent.setdefault(m ^ apart, []).append(swap(after(part, *before) if before else part, "ref", top))

    def mean(m, at):
        theirs = sent[m][0][at]
        if m in last and at.start >= early:
            theirs = sent[m][1][at.start - early : at.stop - early]
        return (0.5 * weights[m][at].astype(F32) + 0.5 * theirs.astype(F32)).astype(BF16)

    score(0)
    singles = [k for k in reversed(range(2, count, 2)) if k & (k - 1) == 0]
    for k in singles:
        pieces[k] = [after(pieces[k][0], weights[0], *(pieces[2 * k + 1] if k != singles[0] else []))]
        pieces[k + 1] = [swap(pieces[k][0], "ref", 1)]
    cut = img_rows * FORWARD_LOW // 8
    for k in range(2, count, 2):
        if k not in singles:
            low, high = k & -k, 1 << (k.bit_length() - 1)
            whole = [jnp.concatenate(pieces[k ^ bit], axis=0) for bit in (low, high)]
            pieces[k] = [swap(whole[0][:cut], "ref", low), swap(whole[1][cut:], "ref", high)]
        if k + 1 not in pieces and k != 2 * end:
            pieces[k + 1] = [swap(part, "ref", 1) for part in pieces[k]]
    send(0, 0, half)
    for m in reversed(range(1, end)):
        score(m)
        send(m, 0, early if m in last else half, *(pieces[3] if m == apart else []))
    sent[apart] = [after(part, *weights.values()) for part in sent[apart]]
    pieces[2 * end] = [after(part, *weights.values()) for part in pieces[2 * end]]
    pieces[2 * end + 1] = [swap(part, "ref", 1) for part in pieces[2 * end]]
    score(end)
    for m in sent:
        if m != apart:
            sent[m] = [after(part, weights[end]) for part in sent[m]]
    send(end, 0, early)

    order = range(blocks)
    every_image = images_of(order)
    scale = 1.0 / jnp.sqrt(F32(total_images))
    def onward(pair, block, bit, before):
        total = pair[0] + after(block, *before).astype(F32)
        return halves(total, "img", bit) if bit < lax.axis_size("img") else (total, total.astype(BF16))

    first, came, pairs = [], [], []
    for c, at in enumerate(chunks):
        w = jnp.concatenate([mean(m, at) for m in order], axis=1)
        w = after(w, *[give for keep, give in first[-1:] + (pairs[-1:] if c > 1 else [])])
        first.append(halves(jnp.dot(w, every_image, preferred_element_type=F32) * scale, "img", 1))
        came.append(swap(first[c][1], "img", 1))
        if c == 0:
            for m in last:
                send(m, early, half, *first[0])
        if c:
            pairs.append(onward(first[c - 1], came[c - 1], 2, [give for keep, give in pairs[-1:]]))
    pairs.append(onward(first[-1], came[-1], 2, [pairs[-1][1]]))
    bit = 2
    while bit < lax.axis_size("img"):
        came = [swap(give, "img", bit) for keep, give in pairs]
        bit *= 2
        after_it = []
        for pair, block in zip(pairs, came):
            after_it.append(onward(pair, block, bit, [give for keep, give in after_it[-1:]]))
        pairs = after_it
    done = [keep for keep, give in pairs]
    gone = [give for keep, give in pairs]
    other = [swap(block, "ref", top).astype(F32) for block in gone]
    return jnp.concatenate(done + other, axis=0).at[place].get(mode="promise_in_bounds")


def solution(mesh):
    in_specs = (P(("img", "ref"), None), P("img"), P("ref", None), P("ref"))
    out_specs = P("ref", "img")
    return jax.shard_map(body, mesh=mesh, in_specs=in_specs, out_specs=out_specs, check_vma=False)
```

```python
import jax
import jax.numpy as jnp
from jax import lax
from jax.sharding import PartitionSpec as P

F32 = jnp.float32
BF16 = jnp.bfloat16
ROW_CHUNKS = (8, 6, 5, 3, 2)
FORWARD_LOW = 9


def swap(block, axis, bit):
    count = lax.axis_size(axis)
    return lax.ppermute(block, axis, [(i, i ^ bit) for i in range(count)])


def after(array, *others):
    return lax.optimization_barrier((array, *others))[0]


def halves(part, axis, bit):
    n = lax.axis_size(axis)
    side = lax.axis_index(axis) // bit % 2
    blocks = n // bit
    width = part.shape[1] // blocks

    def of_side(s):
        cut = [lax.dynamic_slice_in_dim(part, (2 * j + s) * width, width, axis=1) for j in range(blocks // 2)]
        return jnp.concatenate(cut, axis=1)

    return of_side(side), of_side(1 - side).astype(BF16)


def body(images, exponents, references, partners):
    rows, width = references.shape
    half = rows // 2
    count = lax.axis_size("ref")
    me = lax.axis_index("ref")
    img_rows = images.shape[0]
    total_images = img_rows * count * lax.axis_size("img")
    top = count // 2
    upper = me // top

    pieces = {0: [images]}
    for k in reversed(range(2, count, 2)):
        if k & (k - 1) == 0:
            pieces[k] = [swap(images, "ref", k)]
    pieces[1] = [swap(images, "ref", 1)]

    own_order = jnp.arange(rows, dtype=jnp.int32)
    place = jnp.where(upper == 0, own_order, partners % rows)
    place = (place + upper * half) % rows
    one_hot = (own_order[:, None] == place[None, :]).astype(BF16)
    refs = jnp.dot(one_hot, references, preferred_element_type=F32).astype(BF16)
    norms = jnp.sum(jnp.square(refs.astype(F32)), axis=1) / width
    inv_root = 1.0 / jnp.sqrt(F32(width))
    offsets = exponents.reshape(count, img_rows)[me ^ jnp.arange(count)].astype(F32) * 0.25

    apart = top // 2
    blocks = count // 2
    end = blocks - 1
    weights, sent = {}, {}

    def images_of(ms):
        return jnp.concatenate([part for m in ms for k in (2 * m, 2 * m + 1) for part in pieces[k]], axis=0)

    def score(m):
        scores = lax.dot_general(refs, images_of([m]), (((1,), (1,)), ((), ())), preferred_element_type=F32) * inv_root
        scores = scores - 0.5 * norms[:, None] - offsets[2 * m : 2 * m + 2].reshape(1, 2 * img_rows)
        weights[m] = jnp.exp(scores).astype(BF16)

    unit = half // sum(ROW_CHUNKS)
    ends = [0]
    for size in ROW_CHUNKS:
        ends.append(ends[-1] + size * unit)
    chunks = [slice(*pair) for pair in zip(ends, ends[1:])]

    early = ends[1]
    parted = [m for m in range(blocks) if m != apart]

    def send(m, start, stop, *before):
        part = weights[m][half + start : half + stop]
        sent.setdefault(m ^ apart, []).append(swap(after(part, *before) if before else part, "ref", top))

    def mean(m, at):
        theirs = sent[m][0][at]
        if m in parted and at.start >= early:
            theirs = sent[m][1][at.start - early : at.stop - early]
        return (0.5 * weights[m][at].astype(F32) + 0.5 * theirs.astype(F32)).astype(BF16)

    score(0)
    singles = [k for k in reversed(range(2, count, 2)) if k & (k - 1) == 0]
    for k in singles:
        pieces[k] = [after(pieces[k][0], weights[0], *(pieces[2 * k + 1] if k != singles[0] else []))]
        pieces[k + 1] = [swap(pieces[k][0], "ref", 1)]
    cut = img_rows * FORWARD_LOW // 16
    for k in range(2, count, 2):
        if k not in singles:
            low, high = k & -k, 1 << (k.bit_length() - 1)
            whole = [jnp.concatenate(pieces[k ^ bit], axis=0) for bit in (low, high)]
            pieces[k] = [swap(whole[0][:cut], "ref", low), swap(whole[1][cut:], "ref", high)]
        if k + 1 not in pieces and k != 2 * end:
            pieces[k + 1] = [swap(part, "ref", 1) for part in pieces[k]]
    send(0, 0, half, *pieces[3])
    for m in reversed(range(1, end)):
        score(m)
        send(m, 0, early, *(pieces[3] if m == apart else []))
    pieces[2 * end] = [after(part, *weights.values()) for part in pieces[2 * end]]
    pieces[2 * end + 1] = [swap(part, "ref", 1) for part in pieces[2 * end]]
    score(end)
    sent = {m: [after(part, weights[end]) for part in parts] for m, parts in sent.items()}
    send(end, 0, early)

    order = range(blocks)
    every_image = images_of(order)
    scale = 1.0 / jnp.sqrt(F32(total_images))
    def onward(pair, block, bit, before):
        total = pair[0] + after(block, *before).astype(F32)
        return halves(total, "img", bit) if bit < lax.axis_size("img") else (total, total.astype(BF16))

    first, came, pairs = [], [], []
    for c, at in enumerate(chunks):
        w = jnp.concatenate([mean(m, at) for m in order], axis=1)
        w = after(w, *[give for keep, give in first[-1:] + (pairs[-1:] if c > 1 else [])])
        first.append(halves(jnp.dot(w, every_image, preferred_element_type=F32) * scale, "img", 1))
        came.append(swap(first[c][1], "img", 1))
        if c == 0:
            for m in parted:
                send(m ^ apart, early, half, first[0][1])
        if c:
            pairs.append(onward(first[c - 1], came[c - 1], 2, [give for keep, give in pairs[-1:]]))
    pairs.append(onward(first[-1], came[-1], 2, [pairs[-1][1]]))
    bit = 2
    while bit < lax.axis_size("img"):
        came = [swap(give, "img", bit) for keep, give in pairs]
        bit *= 2
        after_it = []
        for pair, block in zip(pairs, came):
            after_it.append(onward(pair, block, bit, [give for keep, give in after_it[-1:]]))
        pairs = after_it
    done = [keep for keep, give in pairs]
    gone = [give for keep, give in pairs]
    other = [swap(block, "ref", top).astype(F32) for block in gone]
    return jnp.concatenate(done + other, axis=0).at[place].get(mode="promise_in_bounds")


def solution(mesh):
    in_specs = (P(("img", "ref"), None), P("img"), P("ref", None), P("ref"))
    out_specs = P("ref", "img")
    return jax.shard_map(body, mesh=mesh, in_specs=in_specs, out_specs=out_specs, check_vma=False)
```

```python
import jax
import jax.numpy as jnp
from jax import lax
from jax.sharding import PartitionSpec as P

F32 = jnp.float32
BF16 = jnp.bfloat16
ROW_CHUNKS = (7, 6, 5, 3, 3)
FORWARD_LOW = 10


def swap(block, axis, bit):
    count = lax.axis_size(axis)
    return lax.ppermute(block, axis, [(i, i ^ bit) for i in range(count)])


def after(array, *others):
    return lax.optimization_barrier((array, *others))[0]


def halves(part, axis, bit):
    n = lax.axis_size(axis)
    side = lax.axis_index(axis) // bit % 2
    blocks = n // bit
    width = part.shape[1] // blocks

    def of_side(s):
        cut = [lax.dynamic_slice_in_dim(part, (2 * j + s) * width, width, axis=1) for j in range(blocks // 2)]
        return jnp.concatenate(cut, axis=1)

    return of_side(side), of_side(1 - side).astype(BF16)


def body(images, exponents, references, partners):
    rows, width = references.shape
    half = rows // 2
    count = lax.axis_size("ref")
    me = lax.axis_index("ref")
    img_rows = images.shape[0]
    total_images = img_rows * count * lax.axis_size("img")
    top = count // 2
    upper = me // top

    pieces = {0: [images]}
    for k in reversed(range(2, count, 2)):
        if k & (k - 1) == 0:
            pieces[k] = [swap(images, "ref", k)]
    pieces[1] = [swap(images, "ref", 1)]

    own_order = jnp.arange(rows, dtype=jnp.int32)
    place = jnp.where(upper == 0, own_order, partners % rows)
    place = (place + upper * half) % rows
    one_hot = (own_order[:, None] == place[None, :]).astype(BF16)
    refs = jnp.dot(one_hot, references, preferred_element_type=F32).astype(BF16)
    norms = jnp.sum(jnp.square(refs.astype(F32)), axis=1) / width
    inv_root = 1.0 / jnp.sqrt(F32(width))
    offsets = exponents.reshape(count, img_rows)[me ^ jnp.arange(count)].astype(F32) * 0.25

    apart = top // 2
    blocks = count // 2
    end = blocks - 1
    weights, sent = {}, {}

    def images_of(ms):
        return jnp.concatenate([part for m in ms for k in (2 * m, 2 * m + 1) for part in pieces[k]], axis=0)

    def score(m):
        scores = lax.dot_general(refs, images_of([m]), (((1,), (1,)), ((), ())), preferred_element_type=F32) * inv_root
        scores = scores - 0.5 * norms[:, None] - offsets[2 * m : 2 * m + 2].reshape(1, 2 * img_rows)
        weights[m] = jnp.exp(scores).astype(BF16)

    unit = half // sum(ROW_CHUNKS)
    ends = [0]
    for size in ROW_CHUNKS:
        ends.append(ends[-1] + size * unit)
    chunks = [slice(*pair) for pair in zip(ends, ends[1:])]

    early = ends[1]
    parted = [m for m in range(blocks) if m != apart]

    def send(m, start, stop, *before):
        part = weights[m][half + start : half + stop]
        sent.setdefault(m ^ apart, []).append(swap(after(part, *before) if before else part, "ref", top))

    def mean(m, at):
        theirs = sent[m][0][at]
        if m in parted and at.start >= early:
            theirs = sent[m][1][at.start - early : at.stop - early]
        return (0.5 * weights[m][at].astype(F32) + 0.5 * theirs.astype(F32)).astype(BF16)

    score(0)
    singles = [k for k in reversed(range(2, count, 2)) if k & (k - 1) == 0]
    for k in singles:
        pieces[k] = [after(pieces[k][0], weights[0], *(pieces[2 * k + 1] if k != singles[0] else []))]
        pieces[k + 1] = [swap(pieces[k][0], "ref", 1)]
    cut = img_rows * FORWARD_LOW // 16
    for k in range(2, count, 2):
        if k not in singles:
            low, high = k & -k, 1 << (k.bit_length() - 1)
            whole = [jnp.concatenate(pieces[k ^ bit], axis=0) for bit in (low, high)]
            pieces[k] = [swap(whole[0][:cut], "ref", low), swap(whole[1][cut:], "ref", high)]
        if k + 1 not in pieces and k != 2 * end:
            pieces[k + 1] = [swap(part, "ref", 1) for part in pieces[k]]
    send(0, 0, half, *pieces[3])
    for m in reversed(range(1, end)):
        score(m)
        send(m, 0, early, *(pieces[3] if m == apart else []))
    pieces[2 * end] = [after(part, *weights.values()) for part in pieces[2 * end]]
    pieces[2 * end + 1] = [swap(part, "ref", 1) for part in pieces[2 * end]]
    score(end)
    sent = {m: [after(part, weights[end]) for part in parts] for m, parts in sent.items()}
    send(end, 0, early)

    order = range(blocks)
    every_image = images_of(order)
    scale = 1.0 / jnp.sqrt(F32(total_images))
    def onward(pair, block, bit, before):
        total = pair[0] + after(block, *before).astype(F32)
        return halves(total, "img", bit) if bit < lax.axis_size("img") else (total, total.astype(BF16))

    first, came, pairs = [], [], []
    for c, at in enumerate(chunks):
        w = jnp.concatenate([mean(m, at) for m in order], axis=1)
        w = after(w, *[give for keep, give in first[-1:] + (pairs[-1:] if 1 < c < len(chunks) - 1 else [])])
        first.append(halves(jnp.dot(w, every_image, preferred_element_type=F32) * scale, "img", 1))
        came.append(swap(first[c][1], "img", 1))
        if c == 0:
            for m in parted:
                send(m ^ apart, early, half, first[0][1])
        if c:
            pairs.append(onward(first[c - 1], came[c - 1], 2, [give for keep, give in pairs[-1:]]))
    pairs.append(onward(first[-1], came[-1], 2, [pairs[-1][1]]))
    bit = 2
    while bit < lax.axis_size("img"):
        came = [swap(give, "img", bit) for keep, give in pairs]
        bit *= 2
        after_it = []
        for pair, block in zip(pairs, came):
            after_it.append(onward(pair, block, bit, [give for keep, give in after_it[-1:]]))
        pairs = after_it
    done = [keep for keep, give in pairs]
    gone = [give for keep, give in pairs]
    other = [swap(block, "ref", top).astype(F32) for block in gone]
    return jnp.concatenate(done + other, axis=0).at[place].get(mode="promise_in_bounds")


def solution(mesh):
    in_specs = (P(("img", "ref"), None), P("img"), P("ref", None), P("ref"))
    out_specs = P("ref", "img")
    return jax.shard_map(body, mesh=mesh, in_specs=in_specs, out_specs=out_specs, check_vma=False)
```

```python
import jax
import jax.numpy as jnp
from jax import lax
from jax.sharding import PartitionSpec as P

F32 = jnp.float32
BF16 = jnp.bfloat16
ROW_CHUNKS = (8, 7, 5, 4)
FORWARD_LOW = 10


def swap(block, axis, bit):
    count = lax.axis_size(axis)
    return lax.ppermute(block, axis, [(i, i ^ bit) for i in range(count)])


def after(array, *others):
    return lax.optimization_barrier((array, *others))[0]


def halves(part, axis, bit):
    n = lax.axis_size(axis)
    side = lax.axis_index(axis) // bit % 2
    blocks = n // bit
    width = part.shape[1] // blocks

    def of_side(s):
        cut = [lax.dynamic_slice_in_dim(part, (2 * j + s) * width, width, axis=1) for j in range(blocks // 2)]
        return jnp.concatenate(cut, axis=1)

    return of_side(side), of_side(1 - side).astype(BF16)


def body(images, exponents, references, partners):
    rows, width = references.shape
    half = rows // 2
    count = lax.axis_size("ref")
    me = lax.axis_index("ref")
    img_rows = images.shape[0]
    total_images = img_rows * count * lax.axis_size("img")
    top = count // 2
    upper = me // top

    pieces = {0: [images]}
    for k in reversed(range(2, count, 2)):
        if k & (k - 1) == 0:
            pieces[k] = [swap(images, "ref", k)]
    pieces[1] = [swap(images, "ref", 1)]

    own_order = jnp.arange(rows, dtype=jnp.int32)
    place = jnp.where(upper == 0, own_order, partners % rows)
    place = (place + upper * half) % rows
    one_hot = (own_order[:, None] == place[None, :]).astype(BF16)
    refs = jnp.dot(one_hot, references, preferred_element_type=F32).astype(BF16)
    norms = jnp.sum(jnp.square(refs.astype(F32)), axis=1) / width
    inv_root = 1.0 / jnp.sqrt(F32(width))
    offsets = exponents.reshape(count, img_rows)[me ^ jnp.arange(count)].astype(F32) * 0.25

    apart = top // 2
    blocks = count // 2
    end = blocks - 1
    weights, sent = {}, {}

    def images_of(ms):
        return jnp.concatenate([part for m in ms for k in (2 * m, 2 * m + 1) for part in pieces[k]], axis=0)

    def score(m):
        scores = lax.dot_general(refs, images_of([m]), (((1,), (1,)), ((), ())), preferred_element_type=F32) * inv_root
        scores = scores - 0.5 * norms[:, None] - offsets[2 * m : 2 * m + 2].reshape(1, 2 * img_rows)
        weights[m] = jnp.exp(scores).astype(BF16)

    unit = half // sum(ROW_CHUNKS)
    ends = [0]
    for size in ROW_CHUNKS:
        ends.append(ends[-1] + size * unit)
    chunks = [slice(*pair) for pair in zip(ends, ends[1:])]

    early = ends[1]
    parted = [m for m in range(blocks) if m != apart]

    def send(m, start, stop, *before):
        part = weights[m][half + start : half + stop]
        sent.setdefault(m ^ apart, []).append(swap(after(part, *before) if before else part, "ref", top))

    def mean(m, at):
        theirs = sent[m][0][at]
        if m in parted and at.start >= early:
            theirs = sent[m][1][at.start - early : at.stop - early]
        return (0.5 * weights[m][at].astype(F32) + 0.5 * theirs.astype(F32)).astype(BF16)

    score(0)
    singles = [k for k in reversed(range(2, count, 2)) if k & (k - 1) == 0]
    for k in singles:
        pieces[k] = [after(pieces[k][0], weights[0], *(pieces[2 * k + 1] if k != singles[0] else []))]
        pieces[k + 1] = [swap(pieces[k][0], "ref", 1)]
    cut = img_rows * FORWARD_LOW // 16
    for k in range(2, count, 2):
        if k not in singles:
            low, high = k & -k, 1 << (k.bit_length() - 1)
            whole = [jnp.concatenate(pieces[k ^ bit], axis=0) for bit in (low, high)]
            pieces[k] = [swap(whole[0][:cut], "ref", low), swap(whole[1][cut:], "ref", high)]
        if k + 1 not in pieces and k != 2 * end:
            pieces[k + 1] = [swap(part, "ref", 1) for part in pieces[k]]
    send(0, 0, half, *pieces[3])
    for m in reversed(range(1, end)):
        score(m)
        if m != 1:
            send(m, 0, early, *(pieces[3] if m == apart else []))
    pieces[2 * end] = [after(part, *weights.values()) for part in pieces[2 * end]]
    pieces[2 * end + 1] = [swap(part, "ref", 1) for part in pieces[2 * end]]
    send(1, 0, early, pieces[2 * end + 1][-1])
    score(end)
    sent = {m: [after(part, weights[end]) for part in parts] for m, parts in sent.items()}
    send(end, 0, early)

    order = range(blocks)
    every_image = images_of(order)
    scale = 1.0 / jnp.sqrt(F32(total_images))
    def onward(pair, block, bit, before):
        total = pair[0] + after(block, *before).astype(F32)
        return halves(total, "img", bit) if bit < lax.axis_size("img") else (total, total.astype(BF16))

    first, came, pairs = [], [], []
    for c, at in enumerate(chunks):
        w = jnp.concatenate([mean(m, at) for m in order], axis=1)
        w = after(w, *[give for keep, give in first[-1:] + (pairs[-1:] if 1 < c < len(chunks) - 1 else [])])
        first.append(halves(jnp.dot(w, every_image, preferred_element_type=F32) * scale, "img", 1))
        came.append(swap(first[c][1], "img", 1))
        if c == 0:
            for m in parted:
                send(m ^ apart, early, half, first[0][1])
        if c:
            pairs.append(onward(first[c - 1], came[c - 1], 2, [give for keep, give in pairs[-1:]]))
    pairs.append(onward(first[-1], came[-1], 2, [pairs[-1][1]]))
    bit = 2
    while bit < lax.axis_size("img"):
        came = [swap(give, "img", bit) for keep, give in pairs]
        bit *= 2
        after_it = []
        for pair, block in zip(pairs, came):
            after_it.append(onward(pair, block, bit, [give for keep, give in after_it[-1:]]))
        pairs = after_it
    done = [keep for keep, give in pairs]
    gone = [give for keep, give in pairs]
    other = [swap(block, "ref", top).astype(F32) for block in gone]
    return jnp.concatenate(done + other, axis=0).at[place].get(mode="promise_in_bounds")


def solution(mesh):
    in_specs = (P(("img", "ref"), None), P("img"), P("ref", None), P("ref"))
    out_specs = P("ref", "img")
    return jax.shard_map(body, mesh=mesh, in_specs=in_specs, out_specs=out_specs, check_vma=False)
```

```python
import jax
import jax.numpy as jnp
from jax import lax
from jax.sharding import PartitionSpec as P

F32 = jnp.float32
BF16 = jnp.bfloat16
ROW_CHUNKS = (8, 7, 5, 4)
FORWARD_LOW = 10


def swap(block, axis, bit):
    count = lax.axis_size(axis)
    return lax.ppermute(block, axis, [(i, i ^ bit) for i in range(count)])


def after(array, *others):
    return lax.optimization_barrier((array, *others))[0]


def halves(part, axis, bit):
    n = lax.axis_size(axis)
    side = lax.axis_index(axis) // bit % 2
    blocks = n // bit
    width = part.shape[1] // blocks

    def of_side(s):
        cut = [lax.dynamic_slice_in_dim(part, (2 * j + s) * width, width, axis=1) for j in range(blocks // 2)]
        return jnp.concatenate(cut, axis=1)

    return of_side(side), of_side(1 - side).astype(BF16)


def body(images, exponents, references, partners):
    rows, width = references.shape
    half = rows // 2
    count = lax.axis_size("ref")
    me = lax.axis_index("ref")
    img_rows = images.shape[0]
    total_images = img_rows * count * lax.axis_size("img")
    top = count // 2
    upper = me // top

    pieces = {0: [images]}
    for k in reversed(range(2, count, 2)):
        if k & (k - 1) == 0:
            pieces[k] = [swap(images, "ref", k)]
    pieces[1] = [swap(images, "ref", 1)]

    own_order = jnp.arange(rows, dtype=jnp.int32)
    place = jnp.where(upper == 0, own_order, partners % rows)
    place = (place + upper * half) % rows
    one_hot = (own_order[:, None] == place[None, :]).astype(BF16)
    refs = jnp.dot(one_hot, references, preferred_element_type=F32).astype(BF16)
    norms = jnp.sum(jnp.square(refs.astype(F32)), axis=1) / width
    inv_root = 1.0 / jnp.sqrt(F32(width))
    offsets = exponents.reshape(count, img_rows)[me ^ jnp.arange(count)].astype(F32) * 0.25

    apart = top // 2
    blocks = count // 2
    end = blocks - 1
    weights, sent = {}, {}

    def images_of(ms):
        return jnp.concatenate([part for m in ms for k in (2 * m, 2 * m + 1) for part in pieces[k]], axis=0)

    def score(m):
        scores = lax.dot_general(refs, images_of([m]), (((1,), (1,)), ((), ())), preferred_element_type=F32) * inv_root
        scores = scores - 0.5 * norms[:, None] - offsets[2 * m : 2 * m + 2].reshape(1, 2 * img_rows)
        weights[m] = jnp.exp(scores).astype(BF16)

    unit = half // sum(ROW_CHUNKS)
    ends = [0]
    for size in ROW_CHUNKS:
        ends.append(ends[-1] + size * unit)
    chunks = [slice(*pair) for pair in zip(ends, ends[1:])]

    early = ends[1]
    parted = [m for m in range(blocks) if m != apart]

    def send(m, start, stop, *before):
        part = weights[m][half + start : half + stop]
        sent.setdefault(m ^ apart, []).append(swap(after(part, *before) if before else part, "ref", top))

    def mean(m, at):
        theirs = sent[m][0][at]
        if m in parted and at.start >= early:
            theirs = sent[m][1][at.start - early : at.stop - early]
        return (0.5 * weights[m][at].astype(F32) + 0.5 * theirs.astype(F32)).astype(BF16)

    score(0)
    singles = [k for k in reversed(range(2, count, 2)) if k & (k - 1) == 0]
    for k in singles:
        pieces[k] = [after(pieces[k][0], weights[0], *(pieces[2 * k + 1] if k != singles[0] else []))]
        pieces[k + 1] = [swap(pieces[k][0], "ref", 1)]
    cut = img_rows * FORWARD_LOW // 16
    for k in range(2, count, 2):
        if k not in singles:
            low, high = k & -k, 1 << (k.bit_length() - 1)
            whole = [jnp.concatenate(pieces[k ^ bit], axis=0) for bit in (low, high)]
            pieces[k] = [swap(whole[0][:cut], "ref", low), swap(whole[1][cut:], "ref", high)]
        if k + 1 not in pieces and k != 2 * end:
            pieces[k + 1] = [swap(part, "ref", 1) for part in pieces[k]]
    send(0, 0, half, *pieces[3])
    for m in reversed(range(1, end)):
        score(m)
        if m != 1:
            send(m, 0, early, *(pieces[3] if m == apart else []))
    pieces[2 * end] = [after(part, *weights.values()) for part in pieces[2 * end]]
    pieces[2 * end + 1] = [swap(part, "ref", 1) for part in pieces[2 * end]]
    send(1, 0, early, pieces[2 * end + 1][-1])
    score(end)
    sent = {m: [after(part, weights[end]) for part in parts] for m, parts in sent.items()}
    send(end, 0, early)

    order = range(blocks)
    every_image = images_of(order)
    scale = 1.0 / jnp.sqrt(F32(total_images))
    def onward(pair, block, bit, before):
        total = pair[0] + after(block, *before).astype(F32)
        return halves(total, "img", bit) if bit < lax.axis_size("img") else (total, total.astype(BF16))

    first, came, pairs = [], [], []
    for c, at in enumerate(chunks):
        w = jnp.concatenate([mean(m, at) for m in order], axis=1)
        w = after(w, *[give for keep, give in first[-1:] + (pairs[-1:] if 1 < c < len(chunks) - 1 else [])])
        first.append(halves(jnp.dot(w, every_image, preferred_element_type=F32) * scale, "img", 1))
        came.append(swap(first[c][1], "img", 1))
        if c == 0:
            for m in parted:
                send(m ^ apart, early, half, first[0][1])
        if c:
            pairs.append(onward(first[c - 1], came[c - 1], 2, [give for keep, give in pairs[-1:]]))
    pairs.append(onward(first[-1], came[-1], 2, [pairs[-1][1]]))
    bit = 2
    while bit < lax.axis_size("img"):
        came = [swap(give, "img", bit) for keep, give in pairs]
        bit *= 2
        after_it = []
        for pair, block in zip(pairs, came):
            after_it.append(onward(pair, block, bit, [give for keep, give in after_it[-1:] + pairs[-1:]]))
        pairs = after_it
    done = [keep for keep, give in pairs]
    gone = [give for keep, give in pairs]
    other = [swap(block, "ref", top).astype(F32) for block in gone]
    return jnp.concatenate(done + other, axis=0).at[place].get(mode="promise_in_bounds")


def solution(mesh):
    in_specs = (P(("img", "ref"), None), P("img"), P("ref", None), P("ref"))
    out_specs = P("ref", "img")
    return jax.shard_map(body, mesh=mesh, in_specs=in_specs, out_specs=out_specs, check_vma=False)
```

```python
import jax
import jax.numpy as jnp
from jax import lax
from jax.sharding import PartitionSpec as P

F32 = jnp.float32
BF16 = jnp.bfloat16
ROW_CHUNKS = (8, 6, 5, 3, 2)
FORWARD_LOW = 10


def swap(block, axis, bit):
    count = lax.axis_size(axis)
    return lax.ppermute(block, axis, [(i, i ^ bit) for i in range(count)])


def after(array, *others):
    return lax.optimization_barrier((array, *others))[0]


def halves(part, axis, bit):
    n = lax.axis_size(axis)
    side = lax.axis_index(axis) // bit % 2
    blocks = n // bit
    width = part.shape[1] // blocks

    def of_side(s):
        cut = [lax.dynamic_slice_in_dim(part, (2 * j + s) * width, width, axis=1) for j in range(blocks // 2)]
        return jnp.concatenate(cut, axis=1)

    return of_side(side), of_side(1 - side).astype(BF16)


def body(images, exponents, references, partners):
    rows, width = references.shape
    half = rows // 2
    count = lax.axis_size("ref")
    me = lax.axis_index("ref")
    img_rows = images.shape[0]
    total_images = img_rows * count * lax.axis_size("img")
    top = count // 2
    upper = me // top

    pieces = {0: [images]}
    for k in reversed(range(2, count, 2)):
        if k & (k - 1) == 0:
            pieces[k] = [swap(images, "ref", k)]
    pieces[1] = [swap(images, "ref", 1)]

    own_order = jnp.arange(rows, dtype=jnp.int32)
    place = jnp.where(upper == 0, own_order, partners % rows)
    place = (place + upper * half) % rows
    one_hot = (own_order[:, None] == place[None, :]).astype(BF16)
    refs = jnp.dot(one_hot, references, preferred_element_type=F32).astype(BF16)
    norms = jnp.sum(jnp.square(refs.astype(F32)), axis=1) / width
    inv_root = 1.0 / jnp.sqrt(F32(width))
    offsets = exponents.reshape(count, img_rows)[me ^ jnp.arange(count)].astype(F32) * 0.25

    apart = top // 2
    blocks = count // 2
    end = blocks - 1
    weights, sent = {}, {}

    def images_of(ms):
        return jnp.concatenate([part for m in ms for k in (2 * m, 2 * m + 1) for part in pieces[k]], axis=0)

    def score(m):
        scores = lax.dot_general(refs, images_of([m]), (((1,), (1,)), ((), ())), preferred_element_type=F32) * inv_root
        scores = scores - 0.5 * norms[:, None] - offsets[2 * m : 2 * m + 2].reshape(1, 2 * img_rows)
        weights[m] = jnp.exp(scores).astype(BF16)

    unit = half // sum(ROW_CHUNKS)
    ends = [0]
    for size in ROW_CHUNKS:
        ends.append(ends[-1] + size * unit)
    chunks = [slice(*pair) for pair in zip(ends, ends[1:])]

    early = ends[1]
    parted = [m for m in range(blocks) if m != apart]

    def send(m, start, stop, *before):
        part = weights[m][half + start : half + stop]
        sent.setdefault(m ^ apart, []).append(swap(after(part, *before) if before else part, "ref", top))

    def mean(m, at):
        theirs = sent[m][0][at]
        if m in parted and at.start >= early:
            theirs = sent[m][1][at.start - early : at.stop - early]
        return (0.5 * weights[m][at].astype(F32) + 0.5 * theirs.astype(F32)).astype(BF16)

    score(0)
    singles = [k for k in reversed(range(2, count, 2)) if k & (k - 1) == 0]
    for k in singles:
        pieces[k] = [after(pieces[k][0], weights[0], *(pieces[2 * k + 1] if k != singles[0] else []))]
        pieces[k + 1] = [swap(pieces[k][0], "ref", 1)]
    cut = img_rows * FORWARD_LOW // 16
    for k in range(2, count, 2):
        if k not in singles:
            low, high = k & -k, 1 << (k.bit_length() - 1)
            whole = [jnp.concatenate(pieces[k ^ bit], axis=0) for bit in (low, high)]
            pieces[k] = [swap(whole[0][:cut], "ref", low), swap(whole[1][cut:], "ref", high)]
        if k + 1 not in pieces and k != 2 * end:
            pieces[k + 1] = [swap(part, "ref", 1) for part in pieces[k]]
    send(0, 0, half, *pieces[3])
    for m in reversed(range(1, end)):
        score(m)
        if m != 1:
            send(m, 0, early, *(pieces[3] if m == apart else []))
    pieces[2 * end] = [after(part, *weights.values()) for part in pieces[2 * end]]
    pieces[2 * end + 1] = [swap(part, "ref", 1) for part in pieces[2 * end]]
    send(1, 0, early, pieces[2 * end + 1][-1])
    score(end)
    sent = {m: [after(part, weights[end]) for part in parts] for m, parts in sent.items()}
    send(end, 0, early)

    order = range(blocks)
    every_image = images_of(order)
    scale = 1.0 / jnp.sqrt(F32(total_images))
    def onward(pair, block, bit, before):
        total = pair[0] + after(block, *before).astype(F32)
        return halves(total, "img", bit) if bit < lax.axis_size("img") else (total, total.astype(BF16))

    first, came, pairs = [], [], []
    for c, at in enumerate(chunks):
        w = jnp.concatenate([mean(m, at) for m in order], axis=1)
        w = after(w, *[give for keep, give in first[-1:] + (pairs[-1:] if 1 < c < len(chunks) - 1 else [])])
        first.append(halves(jnp.dot(w, every_image, preferred_element_type=F32) * scale, "img", 1))
        came.append(swap(first[c][1], "img", 1))
        if c == 0:
            for m in parted:
                send(m ^ apart, early, half, first[0][1])
        if c:
            pairs.append(onward(first[c - 1], came[c - 1], 2, [give for keep, give in pairs[-1:]]))
    pairs.append(onward(first[-1], came[-1], 2, [pairs[-1][1]]))
    bit = 2
    while bit < lax.axis_size("img"):
        came = [swap(give, "img", bit) for keep, give in pairs]
        bit *= 2
        after_it = []
        for c, (pair, block) in enumerate(zip(pairs, came)):
            after_it.append(onward(pair, block, bit, [give for keep, give in after_it[-1:] + pairs[c + 1 : c + 2]]))
        pairs = after_it
    done = [keep for keep, give in pairs]
    gone = [give for keep, give in pairs]
    other = [swap(block, "ref", top).astype(F32) for block in gone]
    return jnp.concatenate(done + other, axis=0).at[place].get(mode="promise_in_bounds")


def solution(mesh):
    in_specs = (P(("img", "ref"), None), P("img"), P("ref", None), P("ref"))
    out_specs = P("ref", "img")
    return jax.shard_map(body, mesh=mesh, in_specs=in_specs, out_specs=out_specs, check_vma=False)
```

```python
import jax
import jax.numpy as jnp
from jax import lax
from jax.sharding import PartitionSpec as P

F32 = jnp.float32
BF16 = jnp.bfloat16
ROW_CHUNKS = (8, 6, 5, 3, 2)
FORWARD_LOW = 10


def swap(block, axis, bit):
    count = lax.axis_size(axis)
    return lax.ppermute(block, axis, [(i, i ^ bit) for i in range(count)])


def after(array, *others):
    return lax.optimization_barrier((array, *others))[0]


def halves(part, axis, bit):
    n = lax.axis_size(axis)
    side = lax.axis_index(axis) // bit % 2
    blocks = n // bit
    width = part.shape[1] // blocks

    def of_side(s):
        cut = [lax.dynamic_slice_in_dim(part, (2 * j + s) * width, width, axis=1) for j in range(blocks // 2)]
        return jnp.concatenate(cut, axis=1)

    return of_side(side), of_side(1 - side).astype(BF16)


def body(images, exponents, references, partners):
    rows, width = references.shape
    half = rows // 2
    count = lax.axis_size("ref")
    me = lax.axis_index("ref")
    img_rows = images.shape[0]
    total_images = img_rows * count * lax.axis_size("img")
    top = count // 2
    upper = me // top

    pieces = {0: [images]}
    for k in reversed(range(2, count, 2)):
        if k & (k - 1) == 0:
            pieces[k] = [swap(images, "ref", k)]
    pieces[1] = [swap(images, "ref", 1)]

    own_order = jnp.arange(rows, dtype=jnp.int32)
    place = jnp.where(upper == 0, own_order, partners % rows)
    place = (place + upper * half) % rows
    one_hot = (own_order[:, None] == place[None, :]).astype(BF16)
    refs = jnp.dot(one_hot, references, preferred_element_type=F32).astype(BF16)
    norms = jnp.sum(jnp.square(refs.astype(F32)), axis=1) / width
    inv_root = 1.0 / jnp.sqrt(F32(width))
    offsets = exponents.reshape(count, img_rows)[me ^ jnp.arange(count)].astype(F32) * 0.25

    apart = top // 2
    blocks = count // 2
    end = blocks - 1
    weights, sent = {}, {}

    def images_of(ms):
        return jnp.concatenate([part for m in ms for k in (2 * m, 2 * m + 1) for part in pieces[k]], axis=0)

    def score(m):
        scores = lax.dot_general(refs, images_of([m]), (((1,), (1,)), ((), ())), preferred_element_type=F32) * inv_root
        scores = scores - 0.5 * norms[:, None] - offsets[2 * m : 2 * m + 2].reshape(1, 2 * img_rows)
        weights[m] = jnp.exp(scores).astype(BF16)

    unit = half // sum(ROW_CHUNKS)
    ends = [0]
    for size in ROW_CHUNKS:
        ends.append(ends[-1] + size * unit)
    chunks = [slice(*pair) for pair in zip(ends, ends[1:])]

    early = ends[1]
    parted = [m for m in range(blocks) if m != apart]

    def send(m, start, stop, *before):
        part = weights[m][half + start : half + stop]
        sent.setdefault(m ^ apart, []).append(swap(after(part, *before) if before else part, "ref", top))

    def mean(m, at):
        theirs = sent[m][0][at]
        if m in parted and at.start >= early:
            theirs = sent[m][1][at.start - early : at.stop - early]
        return (0.5 * weights[m][at].astype(F32) + 0.5 * theirs.astype(F32)).astype(BF16)

    score(0)
    singles = [k for k in reversed(range(2, count, 2)) if k & (k - 1) == 0]
    for k in singles:
        pieces[k] = [after(pieces[k][0], weights[0], *(pieces[2 * k + 1] if k != singles[0] else []))]
        pieces[k + 1] = [swap(pieces[k][0], "ref", 1)]
    cut = img_rows * FORWARD_LOW // 16
    for k in range(2, count, 2):
        if k not in singles:
            low, high = k & -k, 1 << (k.bit_length() - 1)
            whole = [jnp.concatenate(pieces[k ^ bit], axis=0) for bit in (low, high)]
            pieces[k] = [swap(whole[0][:cut], "ref", low), swap(whole[1][cut:], "ref", high)]
        if k + 1 not in pieces and k != 2 * end:
            pieces[k + 1] = [swap(part, "ref", 1) for part in pieces[k]]
    send(0, 0, half, *pieces[3])
    pieces[top + 1] = [after(part, *pieces[3]) for part in pieces[top + 1]]
    for m in reversed(range(1, end)):
        score(m)
        if m != 1:
            send(m, 0, early, *(pieces[3] if m == apart else []))
    pieces[2 * end] = [after(part, *weights.values()) for part in pieces[2 * end]]
    pieces[2 * end + 1] = [swap(part, "ref", 1) for part in pieces[2 * end]]
    send(1, 0, early, pieces[2 * end + 1][-1])
    score(end)
    sent = {m: [after(part, weights[end]) for part in parts] for m, parts in sent.items()}
    send(end, 0, early)

    order = range(blocks)
    every_image = images_of(order)
    scale = 1.0 / jnp.sqrt(F32(total_images))
    def onward(pair, block, bit, before):
        total = pair[0] + after(block, *before).astype(F32)
        return halves(total, "img", bit) if bit < lax.axis_size("img") else (total, total.astype(BF16))

    first, came, pairs = [], [], []
    for c, at in enumerate(chunks):
        w = jnp.concatenate([mean(m, at) for m in order], axis=1)
        w = after(w, *[give for keep, give in first[-1:] + (pairs[-1:] if 1 < c < len(chunks) - 1 else [])])
        first.append(halves(jnp.dot(w, every_image, preferred_element_type=F32) * scale, "img", 1))
        came.append(swap(first[c][1], "img", 1))
        if c == 0:
            for m in parted:
                send(m ^ apart, early, half, first[0][1])
        if c:
            pairs.append(onward(first[c - 1], came[c - 1], 2, [give for keep, give in pairs[-1:]]))
    pairs.append(onward(first[-1], came[-1], 2, [pairs[-1][1]]))
    bit = 2
    while bit < lax.axis_size("img"):
        came = [swap(give, "img", bit) for keep, give in pairs]
        bit *= 2
        after_it = []
        for c, (pair, block) in enumerate(zip(pairs, came)):
            after_it.append(onward(pair, block, bit, [give for keep, give in after_it[-1:] + pairs[c + 1 : c + 2]]))
        pairs = after_it
    done = [keep for keep, give in pairs]
    gone = [give for keep, give in pairs]
    other = [swap(block, "ref", top).astype(F32) for block in gone]
    return jnp.concatenate(done + other, axis=0).at[place].get(mode="promise_in_bounds")


def solution(mesh):
    in_specs = (P(("img", "ref"), None), P("img"), P("ref", None), P("ref"))
    out_specs = P("ref", "img")
    return jax.shard_map(body, mesh=mesh, in_specs=in_specs, out_specs=out_specs, check_vma=False)
```

```python
import jax
import jax.numpy as jnp
from jax import lax
from jax.sharding import PartitionSpec as P

F32 = jnp.float32
BF16 = jnp.bfloat16
ROW_CHUNKS = (8, 6, 5, 3, 2)
FORWARD_LOW = 10


def swap(block, axis, bit):
    count = lax.axis_size(axis)
    return lax.ppermute(block, axis, [(i, i ^ bit) for i in range(count)])


def after(array, *others):
    return lax.optimization_barrier((array, *others))[0]


def halves(part, axis, bit):
    n = lax.axis_size(axis)
    side = lax.axis_index(axis) // bit % 2
    blocks = n // bit
    width = part.shape[1] // blocks

    def of_side(s):
        cut = [lax.dynamic_slice_in_dim(part, (2 * j + s) * width, width, axis=1) for j in range(blocks // 2)]
        return jnp.concatenate(cut, axis=1)

    return of_side(side), of_side(1 - side).astype(BF16)


def body(images, exponents, references, partners):
    rows, width = references.shape
    half = rows // 2
    count = lax.axis_size("ref")
    me = lax.axis_index("ref")
    img_rows = images.shape[0]
    total_images = img_rows * count * lax.axis_size("img")
    top = count // 2
    upper = me // top

    pieces = {0: [images]}
    for k in reversed(range(2, count, 2)):
        if k & (k - 1) == 0:
            pieces[k] = [swap(images, "ref", k)]
    pieces[1] = [swap(images, "ref", 1)]

    own_order = jnp.arange(rows, dtype=jnp.int32)
    place = jnp.where(upper == 0, own_order, partners % rows)
    place = (place + upper * half) % rows
    one_hot = (own_order[:, None] == place[None, :]).astype(BF16)
    refs = jnp.dot(one_hot, references, preferred_element_type=F32).astype(BF16)
    norms = jnp.sum(jnp.square(refs.astype(F32)), axis=1) / width
    inv_root = 1.0 / jnp.sqrt(F32(width))
    offsets = exponents.reshape(count, img_rows)[me ^ jnp.arange(count)].astype(F32) * 0.25

    apart = top // 2
    blocks = count // 2
    end = blocks - 1
    weights, sent = {}, {}

    def images_of(ms):
        return jnp.concatenate([part for m in ms for k in (2 * m, 2 * m + 1) for part in pieces[k]], axis=0)

    def score(m):
        scores = lax.dot_general(refs, images_of([m]), (((1,), (1,)), ((), ())), preferred_element_type=F32) * inv_root
        scores = scores - 0.5 * norms[:, None] - offsets[2 * m : 2 * m + 2].reshape(1, 2 * img_rows)
        weights[m] = jnp.exp(scores).astype(BF16)

    unit = half // sum(ROW_CHUNKS)
    ends = [0]
    for size in ROW_CHUNKS:
        ends.append(ends[-1] + size * unit)
    chunks = [slice(*pair) for pair in zip(ends, ends[1:])]

    early = ends[1]
    parted = [m for m in range(blocks) if m != apart]

    def send(m, start, stop, *before):
        part = weights[m][half + start : half + stop]
        sent.setdefault(m ^ apart, []).append(swap(after(part, *before) if before else part, "ref", top))

    def mean(m, at):
        theirs = sent[m][0][at]
        if m in parted and at.start >= early:
            theirs = sent[m][1][at.start - early : at.stop - early]
        return (0.5 * weights[m][at].astype(F32) + 0.5 * theirs.astype(F32)).astype(BF16)

    score(0)
    singles = [k for k in reversed(range(2, count, 2)) if k & (k - 1) == 0]
    for k in singles:
        pieces[k] = [after(pieces[k][0], weights[0], *(pieces[2 * k + 1] if k != singles[0] else []))]
        pieces[k + 1] = [swap(pieces[k][0], "ref", 1)]
    cut = img_rows * FORWARD_LOW // 16
    for k in range(2, count, 2):
        if k not in singles:
            low, high = k & -k, 1 << (k.bit_length() - 1)
            whole = [jnp.concatenate(pieces[k ^ bit], axis=0) for bit in (low, high)]
            pieces[k] = [swap(whole[0][:cut], "ref", low), swap(whole[1][cut:], "ref", high)]
        if k + 1 not in pieces and k != 2 * end:
            pieces[k + 1] = [swap(part, "ref", 1) for part in pieces[k]]
    send(0, 0, half, *pieces[3])
    for m in reversed(range(1, end)):
        score(m)
        if m != 1:
            send(m, 0, early, *(pieces[3] if m == apart else []))
    pieces[2 * end] = [after(part, *weights.values()) for part in pieces[2 * end]]
    pieces[2 * end + 1] = [swap(part, "ref", 1) for part in pieces[2 * end]]
    send(1, 0, early, pieces[2 * end + 1][-1])
    score(end)
    sent = {m: [after(part, weights[end]) for part in parts] for m, parts in sent.items()}
    send(end, 0, early)

    order = range(blocks)
    every_image = images_of(order)
    scale = 1.0 / jnp.sqrt(F32(total_images))
    def onward(pair, block, bit, before):
        total = pair[0] + after(block, *before).astype(F32)
        return halves(total, "img", bit) if bit < lax.axis_size("img") else (total, total.astype(BF16))

    def gives(*cut):
        return [give for keep, give in cut]

    first, pairs, second = [], [], []
    came, came_second = [], []

    def begin_second(c):
        before = gives(*pairs[-1:]) + (gives(second[c - 2]) if 2 < c < len(chunks) - 1 else [])
        pairs.append(onward(first[c], came[c], 2, before))
        came_second.append(swap(pairs[c][1], "img", 2))
        if c:
            end_second(c - 1)

    def end_second(c):
        before = gives(*second[-1:], *pairs[c + 1 : c + 2])
        second.append(onward(pairs[c], came_second[c], 4, before))

    for c, at in enumerate(chunks):
        w = jnp.concatenate([mean(m, at) for m in order], axis=1)
        w = after(w, *gives(*first[-1:], *(pairs[-1:] if 1 < c < len(chunks) - 1 else [])))
        first.append(halves(jnp.dot(w, every_image, preferred_element_type=F32) * scale, "img", 1))
        came.append(swap(first[c][1], "img", 1))
        if c == 0:
            for m in parted:
                send(m ^ apart, early, half, first[0][1])
        if c:
            begin_second(c - 1)
    begin_second(len(chunks) - 1)
    end_second(len(chunks) - 1)
    pairs = second
    bit = 4
    while bit < lax.axis_size("img"):
        came = [swap(give, "img", bit) for keep, give in pairs]
        bit *= 2
        pairs = [onward(pair, block, bit, []) for pair, block in zip(pairs, came)]
    done = [keep for keep, give in pairs]
    gone = [give for keep, give in pairs]
    other = [swap(block, "ref", top).astype(F32) for block in gone]
    return jnp.concatenate(done + other, axis=0).at[place].get(mode="promise_in_bounds")


def solution(mesh):
    in_specs = (P(("img", "ref"), None), P("img"), P("ref", None), P("ref"))
    out_specs = P("ref", "img")
    return jax.shard_map(body, mesh=mesh, in_specs=in_specs, out_specs=out_specs, check_vma=False)
```

```python
import jax
import jax.numpy as jnp
from jax import lax
from jax.sharding import PartitionSpec as P

F32 = jnp.float32
BF16 = jnp.bfloat16
ROW_CHUNKS = (8, 7, 4, 3, 2)
FORWARD_LOW = 10


def swap(block, axis, bit):
    count = lax.axis_size(axis)
    return lax.ppermute(block, axis, [(i, i ^ bit) for i in range(count)])


def after(array, *others):
    return lax.optimization_barrier((array, *others))[0]


def halves(part, axis, bit):
    n = lax.axis_size(axis)
    side = lax.axis_index(axis) // bit % 2
    blocks = n // bit
    width = part.shape[1] // blocks

    def of_side(s):
        cut = [lax.dynamic_slice_in_dim(part, (2 * j + s) * width, width, axis=1) for j in range(blocks // 2)]
        return jnp.concatenate(cut, axis=1)

    return of_side(side), of_side(1 - side).astype(BF16)


def body(images, exponents, references, partners):
    rows, width = references.shape
    half = rows // 2
    count = lax.axis_size("ref")
    me = lax.axis_index("ref")
    img_rows = images.shape[0]
    total_images = img_rows * count * lax.axis_size("img")
    top = count // 2
    upper = me // top

    pieces = {0: [images]}
    for k in reversed(range(2, count, 2)):
        if k & (k - 1) == 0:
            pieces[k] = [swap(images, "ref", k)]
    pieces[1] = [swap(images, "ref", 1)]

    own_order = jnp.arange(rows, dtype=jnp.int32)
    place = jnp.where(upper == 0, own_order, partners % rows)
    place = (place + upper * half) % rows
    one_hot = (own_order[:, None] == place[None, :]).astype(BF16)
    refs = jnp.dot(one_hot, references, preferred_element_type=F32).astype(BF16)
    norms = jnp.sum(jnp.square(refs.astype(F32)), axis=1) / width
    inv_root = 1.0 / jnp.sqrt(F32(width))
    offsets = exponents.reshape(count, img_rows)[me ^ jnp.arange(count)].astype(F32) * 0.25

    apart = top // 2
    blocks = count // 2
    end = blocks - 1
    weights, sent = {}, {}

    def images_of(ms):
        return jnp.concatenate([part for m in ms for k in (2 * m, 2 * m + 1) for part in pieces[k]], axis=0)

    def score(m):
        scores = lax.dot_general(refs, images_of([m]), (((1,), (1,)), ((), ())), preferred_element_type=F32) * inv_root
        scores = scores - 0.5 * norms[:, None] - offsets[2 * m : 2 * m + 2].reshape(1, 2 * img_rows)
        weights[m] = jnp.exp(scores).astype(BF16)

    unit = half // sum(ROW_CHUNKS)
    ends = [0]
    for size in ROW_CHUNKS:
        ends.append(ends[-1] + size * unit)
    chunks = [slice(*pair) for pair in zip(ends, ends[1:])]

    early = ends[1]
    parted = [m for m in range(blocks) if m != apart]

    def send(m, start, stop, *before):
        part = weights[m][half + start : half + stop]
        sent.setdefault(m ^ apart, []).append(swap(after(part, *before) if before else part, "ref", top))

    def mean(m, at):
        theirs = sent[m][0][at]
        if m in parted and at.start >= early:
            theirs = sent[m][1][at.start - early : at.stop - early]
        return (0.5 * weights[m][at].astype(F32) + 0.5 * theirs.astype(F32)).astype(BF16)

    score(0)
    singles = [k for k in reversed(range(2, count, 2)) if k & (k - 1) == 0]
    for k in singles:
        pieces[k] = [after(pieces[k][0], weights[0], *(pieces[2 * k + 1] if k != singles[0] else []))]
        pieces[k + 1] = [swap(pieces[k][0], "ref", 1)]
    cut = img_rows * FORWARD_LOW // 16
    for k in range(2, count, 2):
        if k not in singles:
            low, high = k & -k, 1 << (k.bit_length() - 1)
            whole = [jnp.concatenate(pieces[k ^ bit], axis=0) for bit in (low, high)]
            pieces[k] = [swap(whole[0][:cut], "ref", low), swap(whole[1][cut:], "ref", high)]
        if k + 1 not in pieces and k != 2 * end:
            pieces[k + 1] = [swap(part, "ref", 1) for part in pieces[k]]
    send(0, 0, half, *pieces[3])
    for m in reversed(range(1, end)):
        score(m)
        if m != 1:
            send(m, 0, early, *(pieces[3] if m == apart else []))
    pieces[2 * end] = [after(part, *weights.values()) for part in pieces[2 * end]]
    pieces[2 * end + 1] = [swap(part, "ref", 1) for part in pieces[2 * end]]
    send(1, 0, early, pieces[2 * end + 1][-1])
    score(end)
    sent = {m: [after(part, weights[end]) for part in parts] for m, parts in sent.items()}
    send(end, 0, early)

    order = range(blocks)
    every_image = images_of(order)
    scale = 1.0 / jnp.sqrt(F32(total_images))
    def onward(pair, block, bit, before):
        total = pair[0] + after(block, *before).astype(F32)
        return halves(total, "img", bit) if bit < lax.axis_size("img") else (total, total.astype(BF16))

    def gives(*cut):
        return [give for keep, give in cut]

    first, pairs, second = [], [], []
    came, came_second = [], []

    def begin_second(c):
        before = gives(*pairs[-1:]) + (gives(second[c - 2]) if 2 < c < len(chunks) - 1 else [])
        pairs.append(onward(first[c], came[c], 2, before))
        came_second.append(swap(pairs[c][1], "img", 2))
        if c:
            end_second(c - 1)

    def end_second(c):
        before = gives(*second[-1:], *pairs[c + 1 : c + 2])
        second.append(onward(pairs[c], came_second[c], 4, before))

    for c, at in enumerate(chunks):
        w = jnp.concatenate([mean(m, at) for m in order], axis=1)
        w = after(w, *gives(*first[-1:], *(pairs[-1:] if 1 < c < len(chunks) - 1 else [])))
        first.append(halves(jnp.dot(w, every_image, preferred_element_type=F32) * scale, "img", 1))
        came.append(swap(first[c][1], "img", 1))
        if c == 0:
            for m in parted:
                send(m ^ apart, early, half, first[0][1])
        if c:
            begin_second(c - 1)
    begin_second(len(chunks) - 1)
    end_second(len(chunks) - 1)
    pairs = second
    bit = 4
    while bit < lax.axis_size("img"):
        came = [swap(give, "img", bit) for keep, give in pairs]
        bit *= 2
        pairs = [onward(pair, block, bit, []) for pair, block in zip(pairs, came)]
    done = [keep for keep, give in pairs]
    gone = [give for keep, give in pairs]
    other = [swap(block, "ref", top).astype(F32) for block in gone]
    return jnp.concatenate(done + other, axis=0).at[place].get(mode="promise_in_bounds")


def solution(mesh):
    in_specs = (P(("img", "ref"), None), P("img"), P("ref", None), P("ref"))
    out_specs = P("ref", "img")
    return jax.shard_map(body, mesh=mesh, in_specs=in_specs, out_specs=out_specs, check_vma=False)
```

```python
import jax
import jax.numpy as jnp
from jax import lax
from jax.sharding import PartitionSpec as P

F32 = jnp.float32
BF16 = jnp.bfloat16
ROW_CHUNKS = (9, 7, 4, 2, 2)
FORWARD_LOW = 10


def swap(block, axis, bit):
    count = lax.axis_size(axis)
    return lax.ppermute(block, axis, [(i, i ^ bit) for i in range(count)])


def after(array, *others):
    return lax.optimization_barrier((array, *others))[0]


def halves(part, axis, bit):
    n = lax.axis_size(axis)
    side = lax.axis_index(axis) // bit % 2
    blocks = n // bit
    width = part.shape[1] // blocks

    def of_side(s):
        cut = [lax.dynamic_slice_in_dim(part, (2 * j + s) * width, width, axis=1) for j in range(blocks // 2)]
        return jnp.concatenate(cut, axis=1)

    return of_side(side), of_side(1 - side).astype(BF16)


def body(images, exponents, references, partners):
    rows, width = references.shape
    half = rows // 2
    count = lax.axis_size("ref")
    me = lax.axis_index("ref")
    img_rows = images.shape[0]
    total_images = img_rows * count * lax.axis_size("img")
    top = count // 2
    upper = me // top

    pieces = {0: [images]}
    for k in reversed(range(2, count, 2)):
        if k & (k - 1) == 0:
            pieces[k] = [swap(images, "ref", k)]
    pieces[1] = [swap(images, "ref", 1)]

    own_order = jnp.arange(rows, dtype=jnp.int32)
    place = jnp.where(upper == 0, own_order, partners % rows)
    place = (place + upper * half) % rows
    one_hot = (own_order[:, None] == place[None, :]).astype(BF16)
    refs = jnp.dot(one_hot, references, preferred_element_type=F32).astype(BF16)
    norms = jnp.sum(jnp.square(refs.astype(F32)), axis=1) / width
    inv_root = 1.0 / jnp.sqrt(F32(width))
    offsets = exponents.reshape(count, img_rows)[me ^ jnp.arange(count)].astype(F32) * 0.25

    apart = top // 2
    blocks = count // 2
    end = blocks - 1
    weights, sent = {}, {}

    def images_of(ms):
        return jnp.concatenate([part for m in ms for k in (2 * m, 2 * m + 1) for part in pieces[k]], axis=0)

    def score(m):
        scores = lax.dot_general(refs, images_of([m]), (((1,), (1,)), ((), ())), preferred_element_type=F32) * inv_root
        scores = scores - 0.5 * norms[:, None] - offsets[2 * m : 2 * m + 2].reshape(1, 2 * img_rows)
        weights[m] = jnp.exp(scores).astype(BF16)

    unit = half // sum(ROW_CHUNKS)
    ends = [0]
    for size in ROW_CHUNKS:
        ends.append(ends[-1] + size * unit)
    chunks = [slice(*pair) for pair in zip(ends, ends[1:])]

    early = ends[1]
    parted = [m for m in range(blocks) if m != apart]

    def send(m, start, stop, *before):
        part = weights[m][half + start : half + stop]
        sent.setdefault(m ^ apart, []).append(swap(after(part, *before) if before else part, "ref", top))

    def mean(m, at):
        theirs = sent[m][0][at]
        if m in parted and at.start >= early:
            theirs = sent[m][1][at.start - early : at.stop - early]
        return (0.5 * weights[m][at].astype(F32) + 0.5 * theirs.astype(F32)).astype(BF16)

    score(0)
    singles = [k for k in reversed(range(2, count, 2)) if k & (k - 1) == 0]
    for k in singles:
        pieces[k] = [after(pieces[k][0], weights[0], *(pieces[2 * k + 1] if k != singles[0] else []))]
        pieces[k + 1] = [swap(pieces[k][0], "ref", 1)]
    cut = img_rows * FORWARD_LOW // 16
    for k in range(2, count, 2):
        if k not in singles:
            low, high = k & -k, 1 << (k.bit_length() - 1)
            whole = [jnp.concatenate(pieces[k ^ bit], axis=0) for bit in (low, high)]
            pieces[k] = [swap(whole[0][:cut], "ref", low), swap(whole[1][cut:], "ref", high)]
        if k + 1 not in pieces and k != 2 * end:
            pieces[k + 1] = [swap(part, "ref", 1) for part in pieces[k]]
    send(0, 0, half, *pieces[3])
    for m in reversed(range(1, end)):
        score(m)
        if m != 1:
            send(m, 0, early, *(pieces[3] if m == apart else []))
    pieces[2 * end] = [after(part, *weights.values()) for part in pieces[2 * end]]
    pieces[2 * end + 1] = [swap(part, "ref", 1) for part in pieces[2 * end]]
    send(1, 0, early, pieces[2 * end + 1][-1])
    score(end)
    sent = {m: [after(part, weights[end]) for part in parts] for m, parts in sent.items()}
    send(end, 0, early)

    order = range(blocks)
    every_image = images_of(order)
    scale = 1.0 / jnp.sqrt(F32(total_images))
    def onward(pair, block, bit, before):
        total = pair[0] + after(block, *before).astype(F32)
        return halves(total, "img", bit) if bit < lax.axis_size("img") else (total, total.astype(BF16))

    def gives(*cut):
        return [give for keep, give in cut]

    first, pairs, second = [], [], []
    came, came_second = [], []

    def begin_second(c):
        before = gives(*pairs[-1:]) + (gives(second[c - 2]) if 2 < c < len(chunks) - 1 else [])
        pairs.append(onward(first[c], came[c], 2, before))
        came_second.append(swap(pairs[c][1], "img", 2))
        if c:
            end_second(c - 1)

    def end_second(c):
        before = gives(*second[-1:], *pairs[c + 1 : c + 2])
        second.append(onward(pairs[c], came_second[c], 4, before))

    for c, at in enumerate(chunks):
        w = jnp.concatenate([mean(m, at) for m in order], axis=1)
        w = after(w, *gives(*first[-1:], *(pairs[-1:] if 1 < c < len(chunks) - 1 else [])))
        first.append(halves(jnp.dot(w, every_image, preferred_element_type=F32) * scale, "img", 1))
        came.append(swap(first[c][1], "img", 1))
        if c == 0:
            for m in parted:
                send(m ^ apart, early, half, first[0][1])
        if c:
            begin_second(c - 1)
    begin_second(len(chunks) - 1)
    end_second(len(chunks) - 1)
    pairs = second
    bit = 4
    while bit < lax.axis_size("img"):
        came = [swap(give, "img", bit) for keep, give in pairs]
        bit *= 2
        pairs = [onward(pair, block, bit, []) for pair, block in zip(pairs, came)]
    done = [keep for keep, give in pairs]
    gone = [give for keep, give in pairs]
    other = [swap(block, "ref", top).astype(F32) for block in gone]
    return jnp.concatenate(done + other, axis=0).at[place].get(mode="promise_in_bounds")


def solution(mesh):
    in_specs = (P(("img", "ref"), None), P("img"), P("ref", None), P("ref"))
    out_specs = P("ref", "img")
    return jax.shard_map(body, mesh=mesh, in_specs=in_specs, out_specs=out_specs, check_vma=False)
```

```python
import jax
import jax.numpy as jnp
from jax import lax
from jax.sharding import PartitionSpec as P

F32 = jnp.float32
BF16 = jnp.bfloat16
ROW_CHUNKS = (8, 7, 4, 3, 2)
FORWARD_LOW = 10


def swap(block, axis, bit):
    count = lax.axis_size(axis)
    return lax.ppermute(block, axis, [(i, i ^ bit) for i in range(count)])


def after(array, *others):
    return lax.optimization_barrier((array, *others))[0]


def halves(part, axis, bit):
    n = lax.axis_size(axis)
    side = lax.axis_index(axis) // bit % 2
    blocks = n // bit
    width = part.shape[1] // blocks

    def of_side(s):
        cut = [lax.dynamic_slice_in_dim(part, (2 * j + s) * width, width, axis=1) for j in range(blocks // 2)]
        return jnp.concatenate(cut, axis=1)

    return of_side(side), of_side(1 - side).astype(BF16)


def body(images, exponents, references, partners):
    rows, width = references.shape
    half = rows // 2
    count = lax.axis_size("ref")
    me = lax.axis_index("ref")
    img_rows = images.shape[0]
    total_images = img_rows * count * lax.axis_size("img")
    top = count // 2
    upper = me // top

    pieces = {0: [images]}
    for k in reversed(range(2, count, 2)):
        if k & (k - 1) == 0:
            pieces[k] = [swap(images, "ref", k)]
    pieces[1] = [swap(images, "ref", 1)]

    own_order = jnp.arange(rows, dtype=jnp.int32)
    place = jnp.where(upper == 0, own_order, partners % rows)
    place = (place + upper * half) % rows
    one_hot = (own_order[:, None] == place[None, :]).astype(BF16)
    refs = jnp.dot(one_hot, references, preferred_element_type=F32).astype(BF16)
    norms = jnp.sum(jnp.square(refs.astype(F32)), axis=1) / width
    inv_root = 1.0 / jnp.sqrt(F32(width))
    offsets = exponents.reshape(count, img_rows)[me ^ jnp.arange(count)].astype(F32) * 0.25

    apart = top // 2
    blocks = count // 2
    end = blocks - 1
    weights, sent = {}, {}

    def images_of(ms):
        return jnp.concatenate([part for m in ms for k in (2 * m, 2 * m + 1) for part in pieces[k]], axis=0)

    def score(m):
        scores = lax.dot_general(refs, images_of([m]), (((1,), (1,)), ((), ())), preferred_element_type=F32) * inv_root
        scores = scores - 0.5 * norms[:, None] - offsets[2 * m : 2 * m + 2].reshape(1, 2 * img_rows)
        weights[m] = jnp.exp(scores).astype(BF16)

    unit = half // sum(ROW_CHUNKS)
    ends = [0]
    for size in ROW_CHUNKS:
        ends.append(ends[-1] + size * unit)
    chunks = [slice(*pair) for pair in zip(ends, ends[1:])]

    early = ends[1]
    parted = [m for m in range(blocks) if m != apart]

    def send(m, start, stop, *before):
        part = weights[m][half + start : half + stop]
        sent.setdefault(m ^ apart, []).append(swap(after(part, *before) if before else part, "ref", top))

    def mean(m, at):
        theirs = sent[m][0][at]
        if m in parted and at.start >= early:
            theirs = sent[m][1][at.start - early : at.stop - early]
        return (0.5 * weights[m][at].astype(F32) + 0.5 * theirs.astype(F32)).astype(BF16)

    score(0)
    singles = [k for k in reversed(range(2, count, 2)) if k & (k - 1) == 0]
    for k in singles:
        pieces[k] = [after(pieces[k][0], weights[0], *(pieces[2 * k + 1] if k != singles[0] else []))]
        pieces[k + 1] = [swap(pieces[k][0], "ref", 1)]
    cut = img_rows * FORWARD_LOW // 16
    for k in range(2, count, 2):
        if k not in singles:
            low, high = k & -k, 1 << (k.bit_length() - 1)
            whole = [jnp.concatenate(pieces[k ^ bit], axis=0) for bit in (low, high)]
            pieces[k] = [swap(whole[0][:cut], "ref", low), swap(whole[1][cut:], "ref", high)]
        if k + 1 not in pieces and k != 2 * end:
            pieces[k + 1] = [swap(part, "ref", 1) for part in pieces[k]]
    send(0, 0, half, *pieces[3])
    for m in reversed(range(1, end)):
        score(m)
        if m != 1:
            send(m, 0, early, *(pieces[3] if m == apart else []))
    pieces[2 * end] = [after(part, *weights.values()) for part in pieces[2 * end]]
    pieces[2 * end + 1] = [swap(part, "ref", 1) for part in pieces[2 * end]]
    score(end)
    sent = {m: [after(part, weights[end]) for part in parts] for m, parts in sent.items()}
    joint = swap(jnp.concatenate([weights[m][half : half + early] for m in (end, 1)], axis=1), "ref", top)
    sent[end ^ apart] = [joint[:, : 2 * img_rows]]
    sent[1 ^ apart] = [joint[:, 2 * img_rows :]]

    order = range(blocks)
    every_image = images_of(order)
    scale = 1.0 / jnp.sqrt(F32(total_images))
    def onward(pair, block, bit, before):
        total = pair[0] + after(block, *before).astype(F32)
        return halves(total, "img", bit) if bit < lax.axis_size("img") else (total, total.astype(BF16))

    def gives(*cut):
        return [give for keep, give in cut]

    first, pairs, second = [], [], []
    came, came_second = [], []

    def begin_second(c):
        before = gives(*pairs[-1:]) + (gives(second[c - 2]) if 2 < c < len(chunks) - 1 else [])
        pairs.append(onward(first[c], came[c], 2, before))
        came_second.append(swap(pairs[c][1], "img", 2))
        if c:
            end_second(c - 1)

    def end_second(c):
        before = gives(*second[-1:], *pairs[c + 1 : c + 2])
        second.append(onward(pairs[c], came_second[c], 4, before))

    for c, at in enumerate(chunks):
        w = jnp.concatenate([mean(m, at) for m in order], axis=1)
        w = after(w, *gives(*first[-1:], *(pairs[-1:] if 1 < c < len(chunks) - 1 else [])))
        first.append(halves(jnp.dot(w, every_image, preferred_element_type=F32) * scale, "img", 1))
        came.append(swap(first[c][1], "img", 1))
        if c == 0:
            for m in parted:
                send(m ^ apart, early, half, first[0][1])
        if c:
            begin_second(c - 1)
    begin_second(len(chunks) - 1)
    end_second(len(chunks) - 1)
    pairs = second
    bit = 4
    while bit < lax.axis_size("img"):
        came = [swap(give, "img", bit) for keep, give in pairs]
        bit *= 2
        pairs = [onward(pair, block, bit, []) for pair, block in zip(pairs, came)]
    done = [keep for keep, give in pairs]
    gone = [give for keep, give in pairs]
    other = [swap(block, "ref", top).astype(F32) for block in gone]
    return jnp.concatenate(done + other, axis=0).at[place].get(mode="promise_in_bounds")


def solution(mesh):
    in_specs = (P(("img", "ref"), None), P("img"), P("ref", None), P("ref"))
    out_specs = P("ref", "img")
    return jax.shard_map(body, mesh=mesh, in_specs=in_specs, out_specs=out_specs, check_vma=False)
```
